32 devices in a mesh: row: 8 (over z, x), col: 4 (over y, core).
Axes of the slice: x: 2, y: 2, z: 4, core: 2. Of those that a mesh axis runs over, the one named last changes fastest.
Arguments:
- weight: float32 [4096, 4096], P('row', 'col'), may hold values from -6 to 6
- blocks: float32 [5, 4096, 512], P(None, ('row', 'col')), may hold values from -0.2 to 1.2
Outputs:
- merged: float32 [4096, 4096], P('row', 'col')
The draws below stay inside these ranges and needn't reach their ends.
All inputs are finite; a program needn't handle non-finite values.
Results may differ from the reference program's by a relative error of at most 0.00017.
Values sent between devices are 32-bit elements; how exact they have to be, the bound alone decides.
No kernel may reach another device: no remote copies, remote signals or barrier semaphores. Data moves between devices by JAX's collectives and lax.ppermute only.
A program may use at most 64 MiB of HBM per device.

```python
import math
import jax
import jax.numpy as jnp
from jax import lax

BS = 512
HALF = 256
COLS_DEV = 1024
FACTORS = 5
ROWS = 4096
COLUMNS = 4096
N_ROW = 8
N_COL = 4


def draw_blocks(key, part):
    row_index = jnp.arange(ROWS)
    identity = (jnp.arange(BS)[None, :] == (row_index % HALF)[:, None]).astype(jnp.float32)
    random_part = jnp.clip(jax.random.normal(key, (FACTORS, ROWS, BS), jnp.float32), -6.0, 6.0)
    scaled = jnp.clip(random_part * (0.5 / math.sqrt(BS)), -0.2, 0.2)
    return identity[None] + scaled


def block_levels(own_key, extent, pieces, smallest, high):
    level, own = 1.0, jax.random.fold_in(own_key, 6)
    for dim, parts in pieces:
        heights = jnp.exp(jax.random.uniform(jax.random.fold_in(own, dim), (parts,), jnp.float32, smallest / len(pieces), high / len(pieces)))
        level = level * jnp.repeat(heights, extent[dim] // parts).reshape([-1 if axis == dim else 1 for axis in range(len(extent))])
    return level


def noise(stream_key, extent, deviation, reach, shards=(), held_as=jnp.bfloat16):
    gain = block_levels(stream_key, extent, shards, -0.22, 0.18) if shards else 1.0
    drawn = jax.random.normal(stream_key, extent, jnp.float32) * deviation * gain
    return jnp.minimum(jnp.maximum(drawn, -reach), reach).astype(held_as)


def setup_inputs(seed: int = 0) -> dict:
    key_of = jax.random.split(jax.random.key(seed), 3)
    weight = noise(key_of[0], (ROWS, COLUMNS), 1.0, 6.0, ((0, 8), (1, 4)), jnp.float32)
    blocks = draw_blocks(jax.random.fold_in(key_of[2], 71), 0)
    return {"weight": weight, "blocks": blocks}


def reference(weight, blocks):
    bit_count = N_ROW.bit_length() - 1
    column_blocks = weight.reshape(ROWS, N_COL, COLS_DEV).transpose(1, 0, 2)

    def apply_factors(weight_slab):
        for factor in range(FACTORS):
            distance_bit = factor % bit_count
            grouped = weight_slab.reshape(N_ROW // (2 * 2 ** distance_bit), 2, 2 ** distance_bit, 2, HALF, COLS_DEV)
            partner = jnp.flip(grouped, axis=1).reshape(N_ROW, 2, HALF, COLS_DEV)
            resident = weight_slab.reshape(N_ROW, 2, HALF, COLS_DEV)
            coefficients = blocks[factor].reshape(N_ROW, 2, HALF, BS)
            stacked = jnp.concatenate([resident, partner], axis=2)
            updated = jnp.einsum("athj,atjc->athc", coefficients, stacked, precision=lax.Precision.HIGHEST)
            weight_slab = updated.reshape(ROWS, COLS_DEV)
        return weight_slab

    result = lax.map(apply_factors, column_blocks)
    return result.transpose(1, 0, 2).reshape(ROWS, N_COL * COLS_DEV)
```

```python
import functools

import jax
import jax.numpy as jnp
from jax import lax
from jax.experimental import pallas as pl
from jax.experimental.pallas import tpu as pltpu
from jax.sharding import PartitionSpec as P

GROUPS = 2
SPLIT = 4
STAGES = 6
FACTORS_RELAYED = (1, 2)


def partner_route(count, mask):
    return [(low, low ^ mask) for low in range(count) if low ^ mask < count]


def halves_of(values):
    high = values.astype(jnp.bfloat16)
    return high, (values - high.astype(jnp.float32)).astype(jnp.bfloat16)


def product(table, first, second):
    high = jnp.concatenate([first[0], second[0]], axis=0)
    low = jnp.concatenate([first[1], second[1]], axis=0)
    dot = functools.partial(jnp.dot, preferred_element_type=jnp.float32)
    return dot(table[0], high) + (dot(table[0], low) + dot(table[1], high))


def prepare(place, mine, mates):
    count, rows, order = mine.shape

    def kernel(place_ref, mine_ref, mates_ref, *table_refs):
        is_low = place_ref[2] == 0
        for k, table_ref in enumerate(table_refs):
            for side in range(2):
                wanted = mine_ref[k] if side == 0 else mates_ref[k]
                other = mates_ref[k] if side == 0 else mine_ref[k]
                high, low = halves_of(jnp.where(is_low, wanted, other))
                table_ref[0, side * rows : (side + 1) * rows] = high
                table_ref[1, side * rows : (side + 1) * rows] = low

    vmem = pl.BlockSpec(memory_space=pltpu.VMEM)
    return pl.pallas_call(
        kernel,
        out_shape=[jax.ShapeDtypeStruct((2, 2 * rows, order), jnp.bfloat16)] * count,
        in_specs=[pl.BlockSpec(memory_space=pltpu.SMEM), vmem, vmem],
        out_specs=[vmem] * count,
        compiler_params=pltpu.CompilerParams(vmem_limit_bytes=32 * 2**20),
        cost_estimate=pl.CostEstimate(
            flops=0, bytes_accessed=16 * count * rows * order, transcendentals=0
        ),
    )(place, mine, mates)


def step(place, weight, merged, held, arrived, tables, live, shape):
    half, width = shape
    enters, m1, m2, m3, pick, m4, m5 = live
    names, operands = [], []

    def take(name, array):
        names.append(name)
        operands.append(array)

    if m1:
        take("x0", held["x0"])
        take("x0_in", arrived["x0"])
        take("t0", tables[m1[0], 0])
    if m2:
        take("a", held["a"])
        take("o0_in", arrived["o0"])
        take("t1", tables[m2[0], 1])
        take("t1x", tables[m2[0], 1, "far"])
    if m3:
        take("m", held["m"])
        take("m_in", arrived["m"])
        take("t2", tables[m3[0], 2])
        take("t2x", tables[m3[0], 2, "far"])
    if pick:
        take("w", held["w"])
        if not m2:
            take("o0_in", arrived["o0"])
    if m4:
        take("x1", held["x1"])
        take("x1_in", arrived["x1"])
        take("t3", tables[m4[0], 3])
    if m5:
        take("o1", held["o1"])
        take("o1_in", arrived["o1"])
        take("t4", tables[m5[0], 4])

    out_names = []
    if enters:
        out_names.append("x0")
    if m1:
        out_names.append("a")
    if m1 or m3:
        out_names.append("o0")
    if m2:
        out_names.append("m")
    if m3:
        out_names.append("w")
    if pick:
        out_names.append("x1")
    if m4:
        out_names.append("o1")
    sizes = {name: ((2,) if name == "m" else ()) + (half, width) for name in out_names}

    def kernel(place_ref, weight_ref, merged_ref, *refs):
        ins = dict(zip(names, refs))
        refs = refs[len(names) :]
        merged_out, outs = refs[0], dict(zip(out_names, refs[1:]))
        refs = refs[1 + len(out_names) :]
        inner = place_ref[3] == 1

        def region(ref, chunk):
            rows = pl.ds(pl.multiple_of(place_ref[chunk[0]] * half, half), half)
            return ref.at[rows, pl.ds(chunk[1] * width, width)]

        if enters:
            entering = pltpu.make_async_copy(region(weight_ref, enters), outs["x0"], refs[-1].at[0])
            entering.start()
        if m5:
            result = refs[0]
            result[...] = product(
                ins["t4"], halves_of(ins["o1"][...]), halves_of(ins["o1_in"][...])
            )
            leaving = pltpu.make_async_copy(result, region(merged_out, m5), refs[-1].at[1])
            leaving.start()
        if m2 or m3:

            @pl.when(inner)
            def _():
                if m3:
                    mine, far = halves_of(ins["m"][0]), halves_of(ins["m"][1])
                    theirs, theirs_far = halves_of(ins["m_in"][0]), halves_of(ins["m_in"][1])
                    outs["o0"][...] = product(ins["t2x"], far, theirs)
                    outs["w"][...] = product(ins["t2"], mine, theirs_far)
                if m2:
                    mine, far = halves_of(ins["a"][...]), halves_of(ins["o0_in"][...])
                    outs["m"][0] = product(ins["t1"], mine, far)
                    outs["m"][1] = product(ins["t1x"], far, mine)

        if pick:
            outs["x1"][...] = jnp.where(inner, ins["w"][...], ins["o0_in"][...])
        if m4:
            outs["o1"][...] = product(
                ins["t3"], halves_of(ins["x1"][...]), halves_of(ins["x1_in"][...])
            )
        if m1:
            mixed = product(ins["t0"], halves_of(ins["x0"][...]), halves_of(ins["x0_in"][...]))
            outs["a"][...] = mixed

            @pl.when(jnp.logical_not(inner))
            def _():
                outs["o0"][...] = mixed

        if enters:
            entering.wait()
        if m5:
            leaving.wait()

    any_space = pl.BlockSpec(memory_space=pl.ANY)
    vmem = pl.BlockSpec(memory_space=pltpu.VMEM)
    scratch = [pltpu.VMEM((half, width), jnp.float32)] if m5 else []
    products = sum(map(bool, (m1, m2, m2, m3, m3, m4, m5)))
    first_merged = merged is None
    head = [weight] if first_merged else [weight, merged]
    body_of = kernel
    if first_merged:
        body_of = lambda place_ref, weight_ref, *refs: kernel(place_ref, weight_ref, None, *refs)
    merged, *results = pl.pallas_call(
        body_of,
        out_shape=[jax.ShapeDtypeStruct(weight.shape, jnp.float32)]
        + [jax.ShapeDtypeStruct(sizes[name], jnp.float32) for name in out_names],
        in_specs=[pl.BlockSpec(memory_space=pltpu.SMEM)]
        + [any_space] * len(head)
        + [vmem] * len(operands),
        out_specs=[any_space] + [vmem] * len(out_names),
        scratch_shapes=scratch + [pltpu.SemaphoreType.DMA((2,))],
        input_output_aliases={} if first_merged else {2: 0},
        compiler_params=pltpu.CompilerParams(vmem_limit_bytes=32 * 2**20),
        cost_estimate=pl.CostEstimate(
            flops=products * 12 * half * half * width,
            bytes_accessed=4 * half * width * (2 + len(names) + len(out_names)),
            transcendentals=0,
        ),
    )(place, *head, *operands)
    return merged, dict(zip(out_names, results))


def relayed(weight, blocks):
    count = lax.axis_size("row")
    columns = lax.axis_size("col")
    half = blocks.shape[2] // 2
    width = weight.shape[1] // SPLIT
    row, col = lax.axis_index("row"), lax.axis_index("col")
    own = col // 2
    is_inner = lambda r: (r >> 1 & 1) != (r >> 2 & 1)
    inner = jnp.where(is_inner(row), 1, 0)
    place = jnp.stack([own, 1 - own, col % 2, inner]).astype(jnp.int32)

    along_x = partner_route(count, 1)
    out_in = [(r, r ^ 2) for r in range(count) if not is_inner(r)]
    in_out = [(r, r ^ 2) for r in range(count) if is_inner(r)]
    middle = [(r, r ^ 6) for r in range(count) if is_inner(r)]
    cores = partner_route(columns, 1)
    across = partner_route(columns, 2)

    far = lax.ppermute(jnp.stack([blocks[k] for k in FACTORS_RELAYED]), "row", out_in)
    mates = lax.ppermute(blocks, "col", cores)
    across_blocks = lax.ppermute(blocks, "col", across)
    far_mates = lax.ppermute(far, "col", cores)
    across_far = lax.ppermute(far, "col", across)
    across_mates = lax.ppermute(across_blocks, "col", cores)
    across_far_mates = lax.ppermute(across_far, "col", cores)
    tables = {}
    for t, near_pair, far_pair in (
        (0, (blocks, mates), (far, far_mates)),
        (1, (across_blocks, across_mates), (across_far, across_far_mates)),
    ):
        for k, table in enumerate(prepare(place, *near_pair)):
            tables[t, k] = table
        for k, table in zip(FACTORS_RELAYED, prepare(place, *far_pair)):
            tables[t, k, "far"] = table

    per_group = SPLIT // GROUPS
    queues = [
        [(t, group * per_group + piece) for t in range(2) for piece in range(per_group)]
        for group in range(GROUPS)
    ]
    length = len(queues[0])
    merged = None
    held = [{} for _ in queues]
    arrived = [{} for _ in queues]
    for tick in range(length + STAGES):
        for group, queue in enumerate(queues):
            live = [
                queue[tick - stage] if 0 <= tick - stage < length else None
                for stage in range(STAGES + 1)
            ]
            merged, now = step(
                place, weight, merged, held[group], arrived[group], tables, live, (half, width)
            )
            held[group] = now
            enters, m1, m2, m3, pick, m4, m5 = live
            new = {}
            if m2:
                new["m"] = lax.ppermute(now["m"], "row", middle)
            if "o0" in now:
                route = (out_in if m1 else []) + (in_out if m3 else [])
                new["o0"] = lax.ppermute(now["o0"], "row", route)
            if "o1" in now:
                new["o1"] = lax.ppermute(now["o1"], "row", out_in + in_out)
            for name in ("x0", "x1"):
                if name in now:
                    new[name] = lax.ppermute(now[name], "row", along_x)
            arrived[group] = new
    return merged


def plain(weight, blocks):
    count = lax.axis_size("row")
    bit_count = count.bit_length() - 1
    factors = blocks.shape[0]
    half = blocks.shape[2] // 2
    halves = weight.shape[0] // half
    tables = [lax.all_gather(blocks[k], "col", axis=0, tiled=True) for k in range(factors)]
    bands = []
    for t in range(halves):
        rows = slice(t * half, (t + 1) * half)
        held = weight[rows]
        for factor in range(factors):
            table = tables[factor][rows]
            partner = lax.ppermute(held, "row", partner_route(count, 1 << factor % bit_count))
            dot = functools.partial(jnp.dot, precision=lax.Precision.HIGHEST)
            held = dot(table[:, :half], held) + dot(table[:, half:], partner)
        bands.append(held)
    return jnp.concatenate(bands, axis=0)


def body(weight, blocks):
    fits = lax.axis_size("row") == 8 and lax.axis_size("col") == 4
    fits = fits and weight.shape[0] == blocks.shape[2] == 4 * blocks.shape[1]
    return (relayed if fits else plain)(weight, blocks)


def solution(mesh):
    return jax.shard_map(
        body,
        mesh=mesh,
        in_specs=(P("row", "col"), P(None, ("row", "col"), None)),
        out_specs=P("row", "col"),
        check_vma=False,
    )
```

```python
import functools

import jax
import jax.numpy as jnp
from jax import lax
from jax.experimental import pallas as pl
from jax.experimental.pallas import tpu as pltpu
from jax.sharding import PartitionSpec as P

OWN, STAYS, VISITS = "own", "stays", "visits"
CHUNKS = (
    ((1, OWN),) * 2 + ((2, VISITS),) * 4 + ((2, STAYS),) * 2 + ((1, STAYS),) * 2
)
EIGHTHS = 8
GROUPS = 2


def partner_route(count, mask):
    return [(low, low ^ mask) for low in range(count) if low ^ mask < count]


def two_terms(values):
    high = values.astype(jnp.bfloat16)
    return high, (values - high.astype(jnp.float32)).astype(jnp.bfloat16)


def product(table, first, second):
    high = jnp.concatenate([first[0], second[0]], axis=0)
    low = jnp.concatenate([first[1], second[1]], axis=0)
    dot = functools.partial(jnp.dot, preferred_element_type=jnp.float32)
    return dot(table[0], high) + (dot(table[0], low) + dot(table[1], high))


def prepare(place, mine, mates):
    count, rows, order = mine.shape

    def kernel(place_ref, mine_ref, mates_ref, *table_refs):
        is_low = place_ref[2] == 0
        for k, table_ref in enumerate(table_refs):
            for side in range(2):
                wanted = mine_ref[k] if side == 0 else mates_ref[k]
                other = mates_ref[k] if side == 0 else mine_ref[k]
                high, low = two_terms(jnp.where(is_low, wanted, other))
                table_ref[0, side * rows : (side + 1) * rows] = high
                table_ref[1, side * rows : (side + 1) * rows] = low

    vmem = pl.BlockSpec(memory_space=pltpu.VMEM)
    return pl.pallas_call(
        kernel,
        out_shape=[jax.ShapeDtypeStruct((2, 2 * rows, order), jnp.bfloat16)] * count,
        in_specs=[pl.BlockSpec(memory_space=pltpu.SMEM), vmem, vmem],
        out_specs=[vmem] * count,
        compiler_params=pltpu.CompilerParams(vmem_limit_bytes=32 * 2**20),
        cost_estimate=pl.CostEstimate(
            flops=0, bytes_accessed=16 * count * rows * order, transcendentals=0
        ),
    )(place, mine, mates)


class Chunk:
    def __init__(self, index, column, width, kind):
        self.index, self.column, self.width = index, column, width
        self.stays, self.visits = kind == STAYS, kind == VISITS
        self.first = -1 if self.visits else 0
        self.last = {OWN: 6, STAYS: 5, VISITS: 7}[kind]


def sends_of(chunk, stage):
    if stage == -1:
        return [("visit", 1, "across")]
    if stage == 6 and chunk.visits:
        return [("return", 1, "across")]
    if stage == 0:
        return [("x", 1, "x")]
    if stage == 1:
        return [("outer", 1, "inward")]
    if stage == 2:
        return [("middle", 2, "middle")]
    if stage == 3:
        return [("both", 2, "x inner")] if chunk.stays else [("back", 1, "outward")]
    if stage == 4:
        return [("done", 1, "outward")] if chunk.stays else [("x", 1, "x")]
    if stage == 5 and not chunk.stays:
        return [("outer", 1, "swap")]
    return []


def plan_sends(tasks):
    sends = [
        (name, chunk, units, route)
        for stage, chunk in tasks
        for name, units, route in sends_of(chunk, stage)
    ]
    arrays, slots = [], {}
    waiting = {}
    for name, chunk, units, route in sends:
        if route == "inward":
            waiting[chunk.width] = (name, chunk)
    for name, chunk, units, route in sends:
        if route == "inward":
            continue
        partner = None
        if route == "outward" and chunk.width in waiting:
            partner, route = waiting.pop(chunk.width), "swap"
        for index, (width, total, where) in enumerate(arrays):
            if (width, where) == (chunk.width, route):
                break
        else:
            index, total = len(arrays), 0
            arrays.append(None)
        arrays[index] = (chunk.width, total + units, route)
        slots[name, chunk.index] = (index, total)
        if partner:
            slots[partner[0], partner[1].index] = (index, total)
    for width, (name, chunk) in waiting.items():
        slots[name, chunk.index] = (len(arrays), 0)
        arrays.append((width, 1, "inward"))
    return arrays, slots


def step(place, weight, merged, blocks, state, tables, tasks, hands, half):
    arrays, slots = plan_sends(tasks)
    operands, operand_at = [], {}

    def take(array):
        if id(array) not in operand_at:
            operand_at[id(array)] = len(operands)
            operands.append(array)
        return operand_at[id(array)]

    views = {}

    def want(kind, name, chunk, stage, units=1):
        array, first = state[kind, name, chunk.index]
        views[kind, name, chunk.index, stage] = (take(array), first)

    table_at = {}

    def want_table(*key):
        table_at[key] = take(tables[key])

    keeps = []
    for stage, chunk in tasks:
        stays = chunk.stays
        if stage == 0 and chunk.visits:
            want("came", "visit", chunk, stage)
        if stage == 7:
            want("came", "return", chunk, stage)
        if stage == 1:
            want("sent", "x", chunk, stage)
            want("came", "x", chunk, stage)
            want_table(0)
            keeps.append(("mixed", chunk))
        if stage == 2:
            want("kept", "mixed", chunk, stage)
            want("came", "outer", chunk, stage)
            want_table(1)
            want_table(1, "far")
        if stage == 3:
            want("sent", "middle", chunk, stage)
            want("came", "middle", chunk, stage)
            want_table(2)
            want_table(2, "far")
            if not stays:
                keeps.append(("inner", chunk))
        if stage == 4 and not stays:
            want("kept", "inner", chunk, stage)
            want("came", "back", chunk, stage)
        if stage == 4 and stays:
            want("sent", "both", chunk, stage)
            want("came", "both", chunk, stage)
            for factor in (3, 4):
                want_table(factor)
                want_table(factor, "far")
        if stage == 5 and not stays:
            want("sent", "x", chunk, stage)
            want("came", "x", chunk, stage)
            want_table(3)
        if stage == 5 and stays:
            want("came", "done", chunk, stage)
        if stage == 6:
            want("sent", "outer", chunk, stage)
            want("came", "outer", chunk, stage)
            want_table(4)
    stored = [c for s, c in tasks if s == c.last or (s == 4 and c.stays)]
    results = [c for s, c in tasks if (s == 6 and not c.visits) or (s == 4 and c.stays)]
    entering = [c for s, c in tasks if s <= 0]
    whole = {"weight": weight if any(s == c.first for s, c in tasks) else None}
    whole["blocks"] = blocks if hands else None
    whole["merged"] = merged
    whole = {name: array for name, array in whole.items() if array is not None}

    def kernel(*refs):
        refs = list(refs)
        place_ref, refs = refs[0], refs[1:]
        whole_refs, refs = dict(zip(whole, refs)), refs[len(whole) :]
        ins, refs = refs[: len(operands)], refs[len(operands) :]
        merged_ref, refs = refs[0], refs[1:]
        sent, refs = refs[: len(arrays)], refs[len(arrays) :]
        kept, refs = dict(zip(keeps, refs)), refs[len(keeps) :]
        handed, refs = refs[: int(bool(hands))], refs[int(bool(hands)) :]
        result_refs, sems = refs[: len(results)], refs[len(results)]
        inner = place_ref[3] == 1
        outer = place_ref[3] == 0

        def region(ref, chunk):
            rows = pl.ds(pl.multiple_of(place_ref[int(chunk.visits)] * half, half), half)
            return ref.at[rows, pl.ds(chunk.column, chunk.width)]

        def slot(name, chunk, unit=0):
            index, first = slots[name, chunk.index]
            return sent[index].at[first + unit]

        def get(kind, name, chunk, stage, unit=0):
            index, first = views[kind, name, chunk.index, stage]
            return ins[index][first + unit]

        def read(*args):
            return two_terms(get(*args))

        def table(*key):
            return ins[table_at[key]]

        started = []
        for stage, chunk in tasks:
            if stage == chunk.first:
                name = "visit" if chunk.visits else "x"
                started.append((None, region(whole_refs["weight"], chunk), slot(name, chunk)))
            elif stage == 0:
                index, first = views["came", "visit", chunk.index, stage]
                started.append((None, ins[index].at[first], slot("x", chunk)))
            elif stage == 7:
                index, first = views["came", "return", chunk.index, stage]
                started.append((None, ins[index].at[first], region(merged_ref, chunk)))
        if hands:
            first, last = hands
            source = whole_refs["blocks"].at[pl.ds(first, last - first)]
            started.append((None, source, handed[0]))
        for stage, chunk in tasks:
            if stage == 5 and chunk.stays:
                index, first = views["came", "done", chunk.index, stage]
                started.append((outer, ins[index].at[first], region(merged_ref, chunk)))
        moves = []

        def start(condition, source, target):
            move = pltpu.make_async_copy(source, target, sems.at[len(moves)])
            moves.append((condition, move))
            if condition is None:
                move.start()
            else:
                pl.when(condition)(move.start)

        for item in started:
            start(*item)

        result_of = dict(zip([c.index for c in results], result_refs))
        for stage, chunk in sorted(tasks, key=lambda task: task[0] != 2):
            if stage == 2:

                @pl.when(inner)
                def _():
                    mine = read("kept", "mixed", chunk, stage)
                    far = read("came", "outer", chunk, stage)
                    slot("middle", chunk, 0)[...] = product(table(1), mine, far)
                    slot("middle", chunk, 1)[...] = product(table(1, "far"), far, mine)

            if stage == 3:

                @pl.when(inner)
                def _():
                    mine = read("sent", "middle", chunk, stage, 0)
                    far = read("sent", "middle", chunk, stage, 1)
                    theirs = read("came", "middle", chunk, stage, 0)
                    theirs_far = read("came", "middle", chunk, stage, 1)
                    near = product(table(2), mine, theirs_far)
                    away = product(table(2, "far"), far, theirs)
                    if chunk.stays:
                        slot("both", chunk, 0)[...] = near
                        slot("both", chunk, 1)[...] = away
                    else:
                        slot("back", chunk)[...] = away
                        kept["inner", chunk][0] = near

            if stage == 4 and chunk.stays:

                @pl.when(inner)
                def _():
                    halves = []
                    for unit, key in ((0, (3,)), (1, (3, "far"))):
                        mine = read("sent", "both", chunk, stage, unit)
                        theirs = read("came", "both", chunk, stage, unit)
                        halves.append(two_terms(product(table(*key), mine, theirs)))
                    near, away = halves
                    result_of[chunk.index][...] = product(table(4), near, away)
                    slot("done", chunk)[...] = product(table(4, "far"), away, near)

                start(inner, result_of[chunk.index], region(merged_ref, chunk))
            if stage == 4 and not chunk.stays:
                slot("x", chunk)[...] = jnp.where(
                    inner,
                    get("kept", "inner", chunk, stage),
                    get("came", "back", chunk, stage),
                )
            if stage == 5 and not chunk.stays:
                slot("outer", chunk)[...] = product(
                    table(3),
                    read("sent", "x", chunk, stage),
                    read("came", "x", chunk, stage),
                )
            if stage == 6:
                target = slot("return", chunk) if chunk.visits else result_of[chunk.index]
                target[...] = product(
                    table(4),
                    read("sent", "outer", chunk, stage),
                    read("came", "outer", chunk, stage),
                )
                if not chunk.visits:
                    start(None, target, region(merged_ref, chunk))
            if stage == 1:
                mixed = product(
                    table(0),
                    read("sent", "x", chunk, stage),
                    read("came", "x", chunk, stage),
                )
                kept["mixed", chunk][0] = mixed

                @pl.when(outer)
                def _():
                    slot("outer", chunk)[...] = mixed

        for condition, move in moves:
            if condition is None:
                move.wait()
            else:
                pl.when(condition)(move.wait)

    hbm = pl.BlockSpec(memory_space=pltpu.HBM)
    vmem = pl.BlockSpec(memory_space=pltpu.VMEM)
    shape_of = lambda units, width: jax.ShapeDtypeStruct((units, half, width), jnp.float32)
    outs = [shape_of(units, width) for width, units, _ in arrays]
    outs += [shape_of(1, chunk.width) for _, chunk in keeps]
    if hands:
        outs.append(jax.ShapeDtypeStruct((hands[1] - hands[0],) + blocks.shape[1:], jnp.float32))
    work = sum(
        chunk.width * {1: 1, 2: 2, 3: 2, 4: 4 * chunk.stays, 5: 1, 6: 1}.get(stage, 0)
        for stage, chunk in tasks
    )
    moved = sum(4 * array.size for array in operands) + sum(4 * out.size for out in outs)
    merged, *made = pl.pallas_call(
        kernel,
        out_shape=[jax.ShapeDtypeStruct(weight.shape, jnp.float32)] + outs,
        in_specs=[pl.BlockSpec(memory_space=pltpu.SMEM)]
        + [hbm] * len(whole)
        + [vmem] * len(operands),
        out_specs=[hbm] + [vmem] * len(outs),
        scratch_shapes=[pltpu.VMEM((half, chunk.width), jnp.float32) for chunk in results]
        + [pltpu.SemaphoreType.DMA((len(entering) + len(stored) + 1,))],
        input_output_aliases={len(whole): 0} if merged is not None else {},
        compiler_params=pltpu.CompilerParams(vmem_limit_bytes=40 * 2**20),
        cost_estimate=pl.CostEstimate(
            flops=12 * half * half * work, bytes_accessed=moved, transcendentals=0
        ),
    )(place, *whole.values(), *operands)
    sent, made = made[: len(arrays)], made[len(arrays) :]
    kept, handed = made[: len(keeps)], made[-1] if hands else None
    now = {}
    for (name, index), (at, first) in slots.items():
        now["sent", name, index] = (sent[at], first)
    for (name, chunk), array in zip(keeps, kept):
        now["kept", name, chunk.index] = (array, 0)
    routes = [route for _, _, route in arrays]
    return merged, now, sent, routes, slots, handed


def relayed(weight, blocks):
    count = lax.axis_size("row")
    columns = lax.axis_size("col")
    half = blocks.shape[2] // 2
    row, col = lax.axis_index("row"), lax.axis_index("col")
    own = col // 2
    is_inner = lambda r: (r >> 1 & 1) != (r >> 2 & 1)
    inner = jnp.where(is_inner(row), 1, 0)
    place = jnp.stack([own, 1 - own, col % 2, inner]).astype(jnp.int32)

    inward = [(r, r ^ 2) for r in range(count) if not is_inner(r)]
    outward = [(r, r ^ 2) for r in range(count) if is_inner(r)]
    route_of = {
        "x": partner_route(count, 1),
        "x inner": [(r, r ^ 1) for r in range(count) if is_inner(r)],
        "inward": inward,
        "outward": outward,
        "swap": inward + outward,
        "middle": [(r, r ^ 6) for r in range(count) if is_inner(r)],
    }
    route_across = partner_route(columns, 2)
    from_core = lambda array: lax.ppermute(array, "col", partner_route(columns, 1))
    tables = {}

    def tabulate(keys, mine):
        for key, table in zip(keys, prepare(place, mine, from_core(mine))):
            tables[key] = table

    chunks, column = [], {True: 0, False: 0}
    for index, (eighths, kind) in enumerate(CHUNKS):
        width = weight.shape[1] * eighths // EIGHTHS
        chunks.append(Chunk(index, column[kind == VISITS], width, kind))
        column[kind == VISITS] += width
    queues = [chunks[group::GROUPS] for group in range(GROUPS)]
    ticks = max(tick + chunk.last for queue in queues for tick, chunk in enumerate(queue)) + 1

    tabulate([(k,) for k in range(blocks.shape[0])], blocks)
    merged = None
    states = [{} for _ in queues]
    copies = {(0, 0): (1, 2), (1, 1): (2, 3), (2, 1): (3, 5)}

    for tick in range(ticks):
        for group, queue in enumerate(queues):
            tasks = [
                (tick - place_in, chunk)
                for place_in, chunk in enumerate(queue)
                if chunk.first <= tick - place_in <= chunk.last
            ]
            if not tasks:
                continue
            merged, now, sent, routes, slots, handed = step(
                place,
                weight,
                merged,
                blocks,
                states[group],
                tables,
                tasks,
                copies.get((tick, group)),
                half,
            )
            order = sorted(range(len(sent)), key=lambda i: routes[i] != "middle")
            came = {}
            for i in order:
                if routes[i] == "across":
                    came[i] = lax.ppermute(sent[i], "col", route_across)
                else:
                    came[i] = lax.ppermute(sent[i], "row", route_of[routes[i]])
            for (name, index), (at, first) in slots.items():
                now["came", name, index] = (came[at], first)
            states[group] = now
            if handed is not None:
                first, last = copies[tick, group]
                far = lax.ppermute(handed, "row", inward)
                tabulate([(k, "far") for k in range(first, last)], far)
    return merged


def plain(weight, blocks):
    count = lax.axis_size("row")
    bit_count = count.bit_length() - 1
    factors = blocks.shape[0]
    half = blocks.shape[2] // 2
    halves = weight.shape[0] // half
    tables = [lax.all_gather(blocks[k], "col", axis=0, tiled=True) for k in range(factors)]
    bands = []
    for t in range(halves):
        rows = slice(t * half, (t + 1) * half)
        held = weight[rows]
        for factor in range(factors):
            table = tables[factor][rows]
            partner = lax.ppermute(held, "row", partner_route(count, 1 << factor % bit_count))
            dot = functools.partial(jnp.dot, precision=lax.Precision.HIGHEST)
            held = dot(table[:, :half], held) + dot(table[:, half:], partner)
        bands.append(held)
    return jnp.concatenate(bands, axis=0)


def body(weight, blocks):
    fits = lax.axis_size("row") == 8 and lax.axis_size("col") == 4 and blocks.shape[0] == 5
    fits = fits and weight.shape[0] == blocks.shape[2] == 4 * blocks.shape[1]
    fits = fits and weight.shape[1] % (128 * EIGHTHS) == 0
    return (relayed if fits else plain)(weight, blocks)


def solution(mesh):
    return jax.shard_map(
        body,
        mesh=mesh,
        in_specs=(P("row", "col"), P(None, ("row", "col"), None)),
        out_specs=P("row", "col"),
        check_vma=False,
    )
```

```python
import functools

import jax
import jax.numpy as jnp
from jax import lax
from jax.experimental import pallas as pl
from jax.experimental.pallas import tpu as pltpu
from jax.sharding import PartitionSpec as P

CHUNKS = ((0, 3), (0, 2), (0, 1), (0, 2), (1, 3), (1, 3), (1, 2))
EIGHTHS = 8
STEPS = (
    (((0, 0),), ("across early",)),
    (((1, 0),), ("near", "across late")),
    (((0, 1), (2, 0)), ()),
    (((1, 1), (3, 0)), ("cores early",)),
    (((0, 2), (2, 1), (4, 0)), ()),
    (((1, 2), (3, 1), (5, 0)), ("far early",)),
    (((2, 2), (4, 1), (6, 0)), ("cores late",)),
    (((0, 3), (3, 2), (5, 1)), ()),
    (((1, 3), (2, 3), (4, 2), (6, 1)), ("far late",)),
    (((0, 4), (3, 3), (5, 2)), ()),
    (((1, 4), (2, 4)), ()),
    (((3, 4), (4, 3), (6, 2)), ()),
    (((0, 5), (1, 5), (5, 3)), ()),
    (((2, 5),), ()),
    (((4, 4),), ()),
    (((6, 3),), ()),
    (((3, 5), (5, 4)), ()),
    (((4, 5), (6, 4)), ()),
    (((5, 5),), ()),
    (((6, 5),), ()),
)
HANDED = {
    "across early": (("blocks", 0, 2), "across"),
    "across late": (("blocks", 2, 5), "across"),
    "cores early": (("across early", 0, 2), "cores"),
    "cores late": (("across late", 0, 3), "cores"),
}
MADE = {
    "near": (0, 0, "blocks", "cores"),
    "far early": (1, 0, "across early", "cores early"),
    "far late": (1, 2, "across late", "cores late"),
}


def partner_route(count, mask):
    return [(low, low ^ mask) for low in range(count) if low ^ mask < count]


def two_terms(values):
    high = values.astype(jnp.bfloat16)
    return high, (values - high.astype(jnp.float32)).astype(jnp.bfloat16)


def product(table, first, second):
    high = jnp.concatenate([first[0], second[0]], axis=0)
    low = jnp.concatenate([first[1], second[1]], axis=0)
    dot = functools.partial(jnp.dot, preferred_element_type=jnp.float32)
    return dot(table[0], high) + (dot(table[0], low) + dot(table[1], high))


class Operands:
    def __init__(self):
        self.arrays, self.places = [], {}

    def add(self, array):
        if id(array) not in self.places:
            self.places[id(array)] = len(self.arrays)
            self.arrays.append(array)
        return self.places[id(array)]


def step(place, weight, blocks, merged, state, tables, rows, tasks, work, chunks, bit_count):
    half = blocks.shape[2] // 2
    stages = blocks.shape[0]
    operands, held, table_at = Operands(), {}, {}
    for index, stage in tasks:
        if stage > 0:
            sent, came = state[index]
            held[index] = [(operands.add(sent[0]), sent[1]), (operands.add(came[0]), came[1])]
            table_at[index] = operands.add(tables[chunks[index][0], stage - 1])
    handing = [name for name in work if name in HANDED]
    making = [name for name in work if name in MADE]
    hand_from = {}
    for name in handing:
        (source, first, last), _ = HANDED[name]
        hand_from[name] = source == "blocks" or operands.add(rows[source])
    make_from = {
        name: [operands.add(rows[source]) for source in MADE[name][2:]] for name in making
    }

    arrays, slots = [], {}
    for index, stage in tasks:
        if stage < stages:
            way = stage % bit_count
            for at, (width, other, total) in enumerate(arrays):
                if (width, other) == (chunks[index][2], way):
                    break
            else:
                at, total = len(arrays), 0
                arrays.append(None)
            arrays[at] = (chunks[index][2], way, total + 1)
            slots[index] = (at, total)
    entering = [index for index, stage in tasks if stage == 0]
    leaving = [index for index, stage in tasks if stage == stages]
    whole = {}
    if entering:
        whole["weight"] = weight
    if True in hand_from.values():
        whole["blocks"] = blocks
    if merged is not None:
        whole["merged"] = merged

    def kernel(*refs):
        place_ref, refs = refs[0], refs[1:]
        whole_refs, refs = dict(zip(whole, refs)), refs[len(whole) :]
        ins, refs = refs[: len(operands.arrays)], refs[len(operands.arrays) :]
        merged_ref, refs = refs[0], refs[1:]
        sends, refs = refs[: len(arrays)], refs[len(arrays) :]
        handed, refs = dict(zip(handing, refs)), refs[len(handing) :]
        made, refs = refs[:made_count], refs[made_count:]
        results, sems = dict(zip(leaving, refs)), refs[len(leaving)]

        def region(ref, index):
            half_block, column, width = chunks[index]
            first = pl.multiple_of(place_ref[half_block] * half, half)
            return ref.at[pl.ds(first, half), pl.ds(column, width)]

        moves = []

        def move(source, target):
            moves.append(pltpu.make_async_copy(source, target, sems.at[len(moves)]))
            moves[-1].start()

        for index in entering:
            at, slot = slots[index]
            move(region(whole_refs["weight"], index), sends[at].at[slot])
        for name in handing:
            (source, first, last), _ = HANDED[name]
            ref = whole_refs["blocks"] if source == "blocks" else ins[hand_from[name]]
            move(ref.at[pl.ds(first, last - first)], handed[name])
        for index, stage in tasks:
            if stage > 0:
                mine, theirs = [two_terms(ins[at][slot]) for at, slot in held[index]]
                if stage == stages:
                    target = results[index]
                else:
                    at, slot = slots[index]
                    target = sends[at].at[slot]
                target[...] = product(ins[table_at[index]], mine, theirs)
                if stage == stages:
                    move(results[index], region(merged_ref, index))
        position = 0
        for name in making:
            mine, mates = [ins[at] for at in make_from[name]]
            low_core = place_ref[2] == 0
            depth = mine.shape[1]
            for k in range(mine.shape[0]):
                for side in range(2):
                    low, high = (mine, mates) if side == 0 else (mates, mine)
                    terms = two_terms(jnp.where(low_core, low[k], high[k]))
                    for term in range(2):
                        made[position][term, side * depth : (side + 1) * depth] = terms[term]
                position += 1
        for each in moves:
            each.wait()

    shape = lambda *dims: jax.ShapeDtypeStruct(dims, jnp.float32)
    outs = [shape(units, half, width) for width, _, units in arrays]
    for name in handing:
        (_, first, last), _ = HANDED[name]
        outs.append(shape(last - first, *blocks.shape[1:]))
    made_keys = [
        (MADE[name][0], MADE[name][1] + k)
        for name in making
        for k in range(rows[MADE[name][2]].shape[0])
    ]
    made_count = len(made_keys)
    outs += [jax.ShapeDtypeStruct((2, half, 2 * half), jnp.bfloat16)] * made_count
    hbm = pl.BlockSpec(memory_space=pltpu.HBM)
    vmem = pl.BlockSpec(memory_space=pltpu.VMEM)
    products = sum(chunks[index][2] for index, stage in tasks if stage > 0)
    merged, *new = pl.pallas_call(
        kernel,
        out_shape=[shape(*weight.shape)] + outs,
        in_specs=[pl.BlockSpec(memory_space=pltpu.SMEM)]
        + [hbm] * len(whole)
        + [vmem] * len(operands.arrays),
        out_specs=[hbm] + [vmem] * len(outs),
        scratch_shapes=[pltpu.VMEM((half, chunks[index][2]), jnp.float32) for index in leaving]
        + [pltpu.SemaphoreType.DMA((len(entering) + len(handing) + len(leaving) + 1,))],
        input_output_aliases={len(whole): 0} if merged is not None else {},
        compiler_params=pltpu.CompilerParams(vmem_limit_bytes=40 * 2**20),
        cost_estimate=pl.CostEstimate(
            flops=12 * half * half * products,
            bytes_accessed=sum(4 * array.size for array in operands.arrays + outs),
            transcendentals=0,
        ),
    )(place, *whole.values(), *operands.arrays)
    sent, new = new[: len(arrays)], new[len(arrays) :]
    handed, made = dict(zip(handing, new)), dict(zip(made_keys, new[len(handing) :]))
    ways = [way for _, way, _ in arrays]
    return merged, sent, ways, slots, handed, made


def pipelined(weight, blocks):
    count, columns = lax.axis_size("row"), lax.axis_size("col")
    bit_count = count.bit_length() - 1
    col = lax.axis_index("col")
    own = col // 2
    place = jnp.stack([own, 1 - own, col % 2]).astype(jnp.int32)
    ways = {
        "cores": partner_route(columns, 1),
        "across": partner_route(columns, 2),
    }
    chunks, column = [], [0, 0]
    for half_block, eighths in CHUNKS:
        width = weight.shape[1] * eighths // EIGHTHS
        chunks.append((half_block, column[half_block], width))
        column[half_block] += width
    rows = {"blocks": blocks, "cores": lax.ppermute(blocks, "col", ways["cores"])}
    merged, state, tables = None, {}, {}
    for tasks, work in STEPS:
        merged, sent, sent_ways, slots, handed, made = step(
            place, weight, blocks, merged, state, tables, rows, tasks, work, chunks, bit_count
        )
        tables.update(made)
        came = [
            lax.ppermute(array, "row", partner_route(count, 1 << way))
            for array, way in zip(sent, sent_ways)
        ]
        for index, (at, slot) in slots.items():
            state[index] = ((sent[at], slot), (came[at], slot))
        for name, array in handed.items():
            rows[name] = lax.ppermute(array, "col", ways[HANDED[name][1]])
    return merged


def plain(weight, blocks):
    count = lax.axis_size("row")
    bit_count = count.bit_length() - 1
    factors = blocks.shape[0]
    half = blocks.shape[2] // 2
    halves = weight.shape[0] // half
    tables = [lax.all_gather(blocks[k], "col", axis=0, tiled=True) for k in range(factors)]
    bands = []
    for t in range(halves):
        rows = slice(t * half, (t + 1) * half)
        held = weight[rows]
        for factor in range(factors):
            table = tables[factor][rows]
            partner = lax.ppermute(held, "row", partner_route(count, 1 << factor % bit_count))
            dot = functools.partial(jnp.dot, precision=lax.Precision.HIGHEST)
            held = dot(table[:, :half], held) + dot(table[:, half:], partner)
        bands.append(held)
    return jnp.concatenate(bands, axis=0)


def body(weight, blocks):
    fits = lax.axis_size("row") == 8 and lax.axis_size("col") == 4 and blocks.shape[0] == 5
    fits = fits and weight.shape[0] == blocks.shape[2] == 4 * blocks.shape[1]
    fits = fits and weight.shape[1] % (128 * EIGHTHS) == 0
    return (pipelined if fits else plain)(weight, blocks)


def solution(mesh):
    return jax.shard_map(
        body,
        mesh=mesh,
        in_specs=(P("row", "col"), P(None, ("row", "col"), None)),
        out_specs=P("row", "col"),
        check_vma=False,
    )
```

```python
import functools

import jax
import jax.numpy as jnp
from jax import lax
from jax.experimental import pallas as pl
from jax.experimental.pallas import tpu as pltpu
from jax.sharding import PartitionSpec as P

CHUNKS = ((0, 2), (0, 2), (0, 4), (1, 4), (1, 2), (1, 2))
EIGHTHS = 8
STEPS = (
    (((0, 0),), ()),
    (((1, 0),), ("across",)),
    ((), ("near",)),
    (((0, 1), (2, 0)), ()),
    (((1, 1),), ()),
    (((0, 2),), ()),
    (((3, 0),), ()),
    (((1, 2),), ()),
    (((2, 1),), ()),
    ((), ("across cores",)),
    (((0, 3),), ()),
    ((), ("far",)),
    (((3, 1), (4, 0)), ()),
    (((0, 4),), ()),
    (((2, 2), (1, 3)), ()),
    (((4, 1),), ()),
    (((3, 2),), ()),
    (((1, 4),), ()),
    (((0, 5), (5, 0)), ()),
    (((5, 1),), ()),
    (((2, 3),), ()),
    (((4, 2),), ()),
    (((2, 4),), ()),
    (((1, 5),), ()),
    (((3, 3),), ()),
    (((5, 2),), ()),
    (((4, 3),), ()),
    (((3, 4),), ()),
    (((2, 5),), ()),
    (((4, 4),), ()),
    (((5, 3),), ()),
    (((5, 4),), ()),
    (((3, 5),), ()),
    (((4, 5),), ()),
    (((5, 5),), ()),
)
HANDED = {
    "across": (("blocks", 0, 5), "across"),
    "across cores": (("across", 0, 5), "cores"),
}
MADE = {
    "near": (0, 0, "blocks", "cores"),
    "far": (1, 0, "across", "across cores"),
}


def partner_route(count, mask):
    return [(low, low ^ mask) for low in range(count) if low ^ mask < count]


def two_terms(values):
    high = values.astype(jnp.bfloat16)
    return high, (values - high.astype(jnp.float32)).astype(jnp.bfloat16)


def product(table, first, second):
    high = jnp.concatenate([first[0], second[0]], axis=0)
    low = jnp.concatenate([first[1], second[1]], axis=0)
    dot = functools.partial(jnp.dot, preferred_element_type=jnp.float32)
    return dot(table[0], high) + (dot(table[0], low) + dot(table[1], high))


class Operands:
    def __init__(self):
        self.arrays, self.places = [], {}

    def add(self, array):
        if id(array) not in self.places:
            self.places[id(array)] = len(self.arrays)
            self.arrays.append(array)
        return self.places[id(array)]


def step(place, weight, blocks, merged, state, tables, rows, tasks, work, chunks, bit_count):
    half = blocks.shape[2] // 2
    stages = blocks.shape[0]
    operands, held, table_at = Operands(), {}, {}
    for index, stage in tasks:
        if stage > 0:
            sent, came = state[index]
            held[index] = [(operands.add(sent[0]), sent[1]), (operands.add(came[0]), came[1])]
            table_at[index] = operands.add(tables[chunks[index][0], stage - 1])
    handing = [name for name in work if name in HANDED]
    making = [name for name in work if name in MADE]
    hand_from = {}
    for name in handing:
        (source, first, last), _ = HANDED[name]
        hand_from[name] = source == "blocks" or operands.add(rows[source])
    make_from = {
        name: [operands.add(rows[source]) for source in MADE[name][2:]] for name in making
    }

    arrays, slots = [], {}
    for index, stage in tasks:
        if stage < stages:
            way = stage % bit_count
            for at, (width, other, total) in enumerate(arrays):
                if (width, other) == (chunks[index][2], way):
                    break
            else:
                at, total = len(arrays), 0
                arrays.append(None)
            arrays[at] = (chunks[index][2], way, total + 1)
            slots[index] = (at, total)
    entering = [index for index, stage in tasks if stage == 0]
    leaving = [index for index, stage in tasks if stage == stages]
    whole = {}
    if entering:
        whole["weight"] = weight
    if True in hand_from.values():
        whole["blocks"] = blocks
    if merged is not None:
        whole["merged"] = merged

    def kernel(*refs):
        place_ref, refs = refs[0], refs[1:]
        whole_refs, refs = dict(zip(whole, refs)), refs[len(whole) :]
        ins, refs = refs[: len(operands.arrays)], refs[len(operands.arrays) :]
        merged_ref, refs = refs[0], refs[1:]
        sends, refs = refs[: len(arrays)], refs[len(arrays) :]
        handed, refs = dict(zip(handing, refs)), refs[len(handing) :]
        made, refs = refs[:made_count], refs[made_count:]
        results, sems = dict(zip(leaving, refs)), refs[len(leaving)]

        def region(ref, index):
            half_block, column, width = chunks[index]
            first = pl.multiple_of(place_ref[half_block] * half, half)
            return ref.at[pl.ds(first, half), pl.ds(column, width)]

        moves = []

        def move(source, target):
            moves.append(pltpu.make_async_copy(source, target, sems.at[len(moves)]))
            moves[-1].start()

        for index in entering:
            at, slot = slots[index]
            move(region(whole_refs["weight"], index), sends[at].at[slot])
        for name in handing:
            (source, first, last), _ = HANDED[name]
            ref = whole_refs["blocks"] if source == "blocks" else ins[hand_from[name]]
            move(ref.at[pl.ds(first, last - first)], handed[name])
        for index, stage in tasks:
            if stage > 0:
                mine, theirs = [two_terms(ins[at][slot]) for at, slot in held[index]]
                if stage == stages:
                    target = results[index]
                else:
                    at, slot = slots[index]
                    target = sends[at].at[slot]
                target[...] = product(ins[table_at[index]], mine, theirs)
                if stage == stages:
                    move(results[index], region(merged_ref, index))
        position = 0
        for name in making:
            mine, mates = [ins[at] for at in make_from[name]]
            low_core = place_ref[2] == 0
            depth = mine.shape[1]
            for k in range(mine.shape[0]):
                for side in range(2):
                    low, high = (mine, mates) if side == 0 else (mates, mine)
                    terms = two_terms(jnp.where(low_core, low[k], high[k]))
                    for term in range(2):
                        made[position][term, side * depth : (side + 1) * depth] = terms[term]
                position += 1
        for each in moves:
            each.wait()

    shape = lambda *dims: jax.ShapeDtypeStruct(dims, jnp.float32)
    outs = [shape(units, half, width) for width, _, units in arrays]
    for name in handing:
        (_, first, last), _ = HANDED[name]
        outs.append(shape(last - first, *blocks.shape[1:]))
    made_keys = [
        (MADE[name][0], MADE[name][1] + k)
        for name in making
        for k in range(rows[MADE[name][2]].shape[0])
    ]
    made_count = len(made_keys)
    outs += [jax.ShapeDtypeStruct((2, half, 2 * half), jnp.bfloat16)] * made_count
    hbm = pl.BlockSpec(memory_space=pltpu.HBM)
    vmem = pl.BlockSpec(memory_space=pltpu.VMEM)
    products = sum(chunks[index][2] for index, stage in tasks if stage > 0)
    merged, *new = pl.pallas_call(
        kernel,
        out_shape=[shape(*weight.shape)] + outs,
        in_specs=[pl.BlockSpec(memory_space=pltpu.SMEM)]
        + [hbm] * len(whole)
        + [vmem] * len(operands.arrays),
        out_specs=[hbm] + [vmem] * len(outs),
        scratch_shapes=[pltpu.VMEM((half, chunks[index][2]), jnp.float32) for index in leaving]
        + [pltpu.SemaphoreType.DMA((len(entering) + len(handing) + len(leaving) + 1,))],
        input_output_aliases={len(whole): 0} if merged is not None else {},
        compiler_params=pltpu.CompilerParams(vmem_limit_bytes=(60 if merged is None else 40) * 2**20),
        cost_estimate=pl.CostEstimate(
            flops=12 * half * half * products,
            bytes_accessed=sum(4 * array.size for array in operands.arrays + outs),
            transcendentals=0,
        ),
    )(place, *whole.values(), *operands.arrays)
    sent, new = new[: len(arrays)], new[len(arrays) :]
    handed, made = dict(zip(handing, new)), dict(zip(made_keys, new[len(handing) :]))
    ways = [way for _, way, _ in arrays]
    return merged, sent, ways, slots, handed, made


def pipelined(weight, blocks):
    count, columns = lax.axis_size("row"), lax.axis_size("col")
    bit_count = count.bit_length() - 1
    col = lax.axis_index("col")
    own = col // 2
    place = jnp.stack([own, 1 - own, col % 2]).astype(jnp.int32)
    ways = {
        "cores": partner_route(columns, 1),
        "across": partner_route(columns, 2),
    }
    chunks, column = [], [0, 0]
    for half_block, eighths in CHUNKS:
        width = weight.shape[1] * eighths // EIGHTHS
        chunks.append((half_block, column[half_block], width))
        column[half_block] += width
    rows = {"blocks": blocks, "cores": lax.ppermute(blocks, "col", ways["cores"])}
    merged, state, tables = None, {}, {}
    for tasks, work in STEPS:
        merged, sent, sent_ways, slots, handed, made = step(
            place, weight, blocks, merged, state, tables, rows, tasks, work, chunks, bit_count
        )
        tables.update(made)
        came = [
            lax.ppermute(array, "row", partner_route(count, 1 << way))
            for array, way in zip(sent, sent_ways)
        ]
        for index, (at, slot) in slots.items():
            state[index] = ((sent[at], slot), (came[at], slot))
        for name, array in handed.items():
            rows[name] = lax.ppermute(array, "col", ways[HANDED[name][1]])
    return merged


def plain(weight, blocks):
    count = lax.axis_size("row")
    bit_count = count.bit_length() - 1
    factors = blocks.shape[0]
    half = blocks.shape[2] // 2
    halves = weight.shape[0] // half
    tables = [lax.all_gather(blocks[k], "col", axis=0, tiled=True) for k in range(factors)]
    bands = []
    for t in range(halves):
        rows = slice(t * half, (t + 1) * half)
        held = weight[rows]
        for factor in range(factors):
            table = tables[factor][rows]
            partner = lax.ppermute(held, "row", partner_route(count, 1 << factor % bit_count))
            dot = functools.partial(jnp.dot, precision=lax.Precision.HIGHEST)
            held = dot(table[:, :half], held) + dot(table[:, half:], partner)
        bands.append(held)
    return jnp.concatenate(bands, axis=0)


def body(weight, blocks):
    fits = lax.axis_size("row") == 8 and lax.axis_size("col") == 4 and blocks.shape[0] == 5
    fits = fits and weight.shape[0] == blocks.shape[2] == 4 * blocks.shape[1]
    fits = fits and weight.shape[1] % (128 * EIGHTHS) == 0
    return (pipelined if fits else plain)(weight, blocks)


def solution(mesh):
    return jax.shard_map(
        body,
        mesh=mesh,
        in_specs=(P("row", "col"), P(None, ("row", "col"), None)),
        out_specs=P("row", "col"),
        check_vma=False,
    )
```

```python
import functools

import jax
import jax.numpy as jnp
from jax import lax
from jax.experimental import pallas as pl
from jax.experimental.pallas import tpu as pltpu
from jax.sharding import PartitionSpec as P

CHUNKS = ((0, 2), (0, 2), (0, 2), (0, 2), (1, 2), (1, 2), (1, 2), (1, 2))
EIGHTHS = 8
STEPS = (
    (((0, 0),), ()),
    (((1, 0),), ()),
    (((0, 1), (2, 0)), ("near",)),
    (((1, 1),), ()),
    (((0, 2),), ()),
    (((2, 1), (3, 0)), ()),
    (((1, 2),), ()),
    (((0, 3),), ()),
    (((2, 2),), ()),
    (((3, 1),), ()),
    (((1, 3),), ()),
    (((0, 4),), ()),
    (((2, 3),), ()),
    (((3, 2),), ()),
    (((1, 4), (0, 5), (4, 0)), ()),
    (((2, 4), (5, 0)), ("far",)),
    (((3, 3), (1, 5)), ()),
    (((4, 1), (6, 0)), ()),
    (((2, 5),), ()),
    (((5, 1), (7, 0)), ()),
    (((4, 2), (3, 4)), ()),
    (((6, 1),), ()),
    (((5, 2),), ()),
    (((7, 1),), ()),
    (((4, 3),), ()),
    (((3, 5),), ()),
    (((6, 2),), ()),
    (((5, 3),), ()),
    (((7, 2),), ()),
    (((4, 4),), ()),
    (((6, 3),), ()),
    (((5, 4),), ()),
    (((7, 3),), ()),
    (((4, 5),), ()),
    (((6, 4),), ()),
    (((5, 5),), ()),
    (((7, 4),), ()),
    (((6, 5),), ()),
    (((7, 5),), ()),
)
NEAR, FAR = "near", "far"


def partner_route(count, mask):
    return [(low, low ^ mask) for low in range(count) if low ^ mask < count]


def two_terms(values):
    high = values.astype(jnp.bfloat16)
    return high, (values - high.astype(jnp.float32)).astype(jnp.bfloat16)


def product(table, first, second):
    high = jnp.concatenate([first[0], second[0]], axis=0)
    low = jnp.concatenate([first[1], second[1]], axis=0)
    dot = functools.partial(jnp.dot, preferred_element_type=jnp.float32)
    return dot(table[0], high) + (dot(table[0], low) + dot(table[1], high))


class Operands:
    def __init__(self):
        self.arrays, self.places = [], {}

    def add(self, array):
        if id(array) not in self.places:
            self.places[id(array)] = len(self.arrays)
            self.arrays.append(array)
        return self.places[id(array)]


def step(place, weight, blocks, merged, state, tables, rows, tasks, work, chunks, bit_count):
    half = blocks.shape[2] // 2
    stages = blocks.shape[0]
    operands, held, table_at = Operands(), {}, {}
    for index, stage in tasks:
        if stage > 0:
            sent, came = state[index]
            held[index] = [(operands.add(sent[0]), sent[1]), (operands.add(came[0]), came[1])]
            key = (chunks[index][0], stage - 1)
            table_at[index] = key if key not in tables else operands.add(tables[key])
    if NEAR in work:
        table_from = [operands.add(rows[name]) for name in ("blocks", "cores")]
    if FAR in work:
        table_from = [operands.add(rows["across"])]

    arrays, slots = [], {}
    for index, stage in tasks:
        if stage < stages:
            way = stage % bit_count
            for at, (width, other, total) in enumerate(arrays):
                if (width, other) == (chunks[index][2], way):
                    break
            else:
                at, total = len(arrays), 0
                arrays.append(None)
            arrays[at] = (chunks[index][2], way, total + 1)
            slots[index] = (at, total)
    entering = [index for index, stage in tasks if stage == 0]
    leaving = [index for index, stage in tasks if stage == stages]
    whole = {}
    if entering:
        whole["weight"] = weight
    if merged is not None:
        whole["merged"] = merged

    def kernel(*refs):
        place_ref, refs = refs[0], refs[1:]
        whole_refs, refs = dict(zip(whole, refs)), refs[len(whole) :]
        ins, refs = refs[: len(operands.arrays)], refs[len(operands.arrays) :]
        merged_ref, refs = refs[0], refs[1:]
        sends, refs = refs[: len(arrays)], refs[len(arrays) :]
        ordered, refs = refs[: int(NEAR in work)], refs[int(NEAR in work) :]
        made, refs = refs[: len(made_keys)], refs[len(made_keys) :]
        results, sems = dict(zip(leaving, refs)), refs[len(leaving)]

        def region(ref, index):
            half_block, column, width = chunks[index]
            first = pl.multiple_of(place_ref[half_block] * half, half)
            return ref.at[pl.ds(first, half), pl.ds(column, width)]

        moves = []

        def move(source, target):
            moves.append(pltpu.make_async_copy(source, target, sems.at[len(moves)]))
            moves[-1].start()

        for index in entering:
            at, slot = slots[index]
            move(region(whole_refs["weight"], index), sends[at].at[slot])
        for k, table in enumerate(made):
            if NEAR in work:
                mine, mates = [ins[at][k] for at in table_from]
                low_core = place_ref[2] == 0
                depth = mine.shape[0]
                ordered[0][k, :depth] = jnp.where(low_core, mine, mates)
                ordered[0][k, depth:] = jnp.where(low_core, mates, mine)
            source = ordered[0] if NEAR in work else ins[table_from[0]]
            table[0], table[1] = two_terms(source[k])
        for index, stage in tasks:
            if stage > 0:
                mine, theirs = [two_terms(ins[at][slot]) for at, slot in held[index]]
                if stage == stages:
                    target = results[index]
                else:
                    at, slot = slots[index]
                    target = sends[at].at[slot]
                at = table_at[index]
                table = ins[at] if isinstance(at, int) else made[made_keys.index(at)]
                target[...] = product(table, mine, theirs)
                if stage == stages:
                    move(results[index], region(merged_ref, index))
        for each in moves:
            each.wait()

    shape = lambda *dims: jax.ShapeDtypeStruct(dims, jnp.float32)
    outs = [shape(units, half, width) for width, _, units in arrays]
    if NEAR in work:
        outs.append(shape(stages, half, 2 * half))
    made_keys = []
    if NEAR in work or FAR in work:
        made_keys = [(int(FAR in work), k) for k in range(stages)]
    outs += [jax.ShapeDtypeStruct((2, half, 2 * half), jnp.bfloat16)] * len(made_keys)
    hbm = pl.BlockSpec(memory_space=pltpu.HBM)
    vmem = pl.BlockSpec(memory_space=pltpu.VMEM)
    merged, *new = pl.pallas_call(
        kernel,
        out_shape=[shape(*weight.shape)] + outs,
        in_specs=[pl.BlockSpec(memory_space=pltpu.SMEM)]
        + [hbm] * len(whole)
        + [vmem] * len(operands.arrays),
        out_specs=[hbm] + [vmem] * len(outs),
        scratch_shapes=[pltpu.VMEM((half, chunks[index][2]), jnp.float32) for index in leaving]
        + [pltpu.SemaphoreType.DMA((len(entering) + len(leaving) + 1,))],
        input_output_aliases={len(whole): 0} if merged is not None else {},
        compiler_params=pltpu.CompilerParams(vmem_limit_bytes=(60 if merged is None else 40) * 2**20),
        cost_estimate=pl.CostEstimate(flops=1, bytes_accessed=1, transcendentals=0),
    )(place, *whole.values(), *operands.arrays)
    sent, new = new[: len(arrays)], new[len(arrays) :]
    ordered = new.pop(0) if NEAR in work else None
    made = dict(zip(made_keys, new))
    ways = [way for _, way, _ in arrays]
    return merged, sent, ways, slots, ordered, made


def pipelined(weight, blocks):
    count, columns = lax.axis_size("row"), lax.axis_size("col")
    bit_count = count.bit_length() - 1
    col = lax.axis_index("col")
    own = col // 2
    place = jnp.stack([own, 1 - own, col % 2]).astype(jnp.int32)
    chunks, column = [], [0, 0]
    for half_block, eighths in CHUNKS:
        width = weight.shape[1] * eighths // EIGHTHS
        chunks.append((half_block, column[half_block], width))
        column[half_block] += width
    rows = {"blocks": blocks, "cores": lax.ppermute(blocks, "col", partner_route(columns, 1))}
    merged, state, tables = None, {}, {}
    for tasks, work in STEPS:
        merged, sent, sent_ways, slots, ordered, made = step(
            place, weight, blocks, merged, state, tables, rows, tasks, work, chunks, bit_count
        )
        tables.update(made)
        came = [
            lax.ppermute(array, "row", partner_route(count, 1 << way))
            for array, way in zip(sent, sent_ways)
        ]
        for index, (at, slot) in slots.items():
            state[index] = ((sent[at], slot), (came[at], slot))
        if ordered is not None:
            rows["across"] = lax.ppermute(ordered, "col", partner_route(columns, 2))
    return merged


def plain(weight, blocks):
    count = lax.axis_size("row")
    bit_count = count.bit_length() - 1
    factors = blocks.shape[0]
    half = blocks.shape[2] // 2
    halves = weight.shape[0] // half
    tables = [lax.all_gather(blocks[k], "col", axis=0, tiled=True) for k in range(factors)]
    bands = []
    for t in range(halves):
        rows = slice(t * half, (t + 1) * half)
        held = weight[rows]
        for factor in range(factors):
            table = tables[factor][rows]
            partner = lax.ppermute(held, "row", partner_route(count, 1 << factor % bit_count))
            dot = functools.partial(jnp.dot, precision=lax.Precision.HIGHEST)
            held = dot(table[:, :half], held) + dot(table[:, half:], partner)
        bands.append(held)
    return jnp.concatenate(bands, axis=0)


def body(weight, blocks):
    fits = lax.axis_size("row") == 8 and lax.axis_size("col") == 4 and blocks.shape[0] == 5
    fits = fits and weight.shape[0] == blocks.shape[2] == 4 * blocks.shape[1]
    fits = fits and weight.shape[1] % (128 * EIGHTHS) == 0
    return (pipelined if fits else plain)(weight, blocks)


def solution(mesh):
    return jax.shard_map(
        body,
        mesh=mesh,
        in_specs=(P("row", "col"), P(None, ("row", "col"), None)),
        out_specs=P("row", "col"),
        check_vma=False,
    )
```

```python
import functools

import jax
import jax.numpy as jnp
from jax import lax
from jax.experimental import pallas as pl
from jax.experimental.pallas import tpu as pltpu
from jax.sharding import PartitionSpec as P

CHUNKS = ((0, 2), (0, 2), (0, 2), (0, 2), (1, 2), (1, 2), (1, 2), (1, 2))
EIGHTHS = 8
STEPS = (
    (((3, 0),), ("across",)),
    (((0, 0),), ("near01",)),
    ((), ("near24",)),
    (((3, 1), (2, 0)), ()),
    (((1, 0), (0, 1), (6, 0)), ()),
    (((3, 2),), ()),
    (((5, 0), (2, 1), (0, 2), (7, 0)), ()),
    (((2, 2), (1, 1), (3, 3)), ("cs0",)),
    (((6, 1), (7, 1), (0, 3), (4, 0)), ("mk0", "cs1")),
    (((1, 2), (5, 1)), ("cs2",)),
    (((2, 3), (5, 2)), ("mk1", "mk2")),
    (((7, 2), (4, 1), (1, 3)), ("cs3",)),
    (((3, 4), (4, 2), (5, 3)), ("cs4",)),
    (((6, 2), (0, 4), (7, 3), (5, 4)), ("mk3",)),
    (((4, 3),), ()),
    (((7, 4), (2, 4), (3, 5)), ()),
    (((1, 4),), ()),
    (((6, 3), (0, 5), (4, 4)), ()),
    (((5, 5), (7, 5), (6, 4), (1, 5)), ("mk4",)),
    (((2, 5), (4, 5)), ()),
    (((6, 5),), ()),
)
NEAR = {"near01": (0, 2), "near24": (2, 5)}
ACROSS = "across"
SHARE = {"cs0": 0, "cs1": 1, "cs2": 2, "cs3": 3, "cs4": 4}
FAR = {"mk0": "cs0", "mk1": "cs1", "mk2": "cs2", "mk3": "cs3", "mk4": "cs4"}


def partner_route(count, mask):
    return [(low, low ^ mask) for low in range(count) if low ^ mask < count]


def two_terms(values):
    high = values.astype(jnp.bfloat16)
    return high, (values - high.astype(jnp.float32)).astype(jnp.bfloat16)


def product(table, first, second):
    high = jnp.concatenate([first[0], second[0]], axis=0)
    low = jnp.concatenate([first[1], second[1]], axis=0)
    dot = functools.partial(jnp.dot, preferred_element_type=jnp.float32)
    return dot(table[0], high) + (dot(table[0], low) + dot(table[1], high))


class Operands:
    def __init__(self):
        self.arrays, self.places = [], {}

    def add(self, array):
        if id(array) not in self.places:
            self.places[id(array)] = len(self.arrays)
            self.arrays.append(array)
        return self.places[id(array)]


def step(weight, blocks, merged, state, tables, rows, tasks, work, chunks, bit_count):
    half = blocks.shape[2] // 2
    stages = blocks.shape[0]
    operands, held, taken = Operands(), {}, {}
    for index, stage in tasks:
        if stage > 0:
            sent, came = state[index]
            held[index] = [(operands.add(sent[0]), sent[1]), (operands.add(came[0]), came[1])]
            key = (chunks[index][0], stage - 1)
            if key in tables:
                taken[key] = operands.add(tables[key])

    making, handing = [], []
    for name in work:
        if name in NEAR:
            mine, other = [operands.add(rows[n]) for n in ("blocks", "cores")]
            making += [((0, k), (mine, k), (other, k)) for k in range(*NEAR[name])]
        elif name in FAR:
            k = SHARE[FAR[name]]
            mine, other = operands.add(rows[ACROSS]), operands.add(rows[FAR[name]])
            making.append(((1, k), (mine, k), (other, 0)))
        elif name == ACROSS:
            handing.append((name, None, 0, stages))
        else:
            handing.append((name, operands.add(rows[ACROSS]), SHARE[name], SHARE[name] + 1))

    arrays, slots = [], {}
    for index, stage in tasks:
        if stage < stages:
            way = stage % bit_count
            for at, (width, other, total) in enumerate(arrays):
                if (width, other) == (chunks[index][2], way):
                    break
            else:
                at, total = len(arrays), 0
                arrays.append(None)
            arrays[at] = (chunks[index][2], way, total + 1)
            slots[index] = (at, total)
    entering = [index for index, stage in tasks if stage == 0]
    leaving = [index for index, stage in tasks if stage == stages]
    whole = {}
    if entering:
        whole["weight"] = weight
    if any(source is None for _, source, _, _ in handing):
        whole["blocks"] = blocks
    if merged is not None:
        whole["merged"] = merged

    def kernel(*refs):
        whole_refs, refs = dict(zip(whole, refs)), refs[len(whole) :]
        ins, refs = refs[: len(operands.arrays)], refs[len(operands.arrays) :]
        merged_ref, refs = refs[0], refs[1:]
        sends, refs = refs[: len(arrays)], refs[len(arrays) :]
        handed, refs = refs[: len(handing)], refs[len(handing) :]
        made, refs = dict(zip([key for key, _, _ in making], refs)), refs[len(making) :]
        result_of, sems = dict(zip(leaving, refs)), refs[len(leaving)]
        col = lax.axis_index("col")
        own_half, low_core = col // 2, col % 2 == 0

        def region(ref, index):
            half_block, column, width = chunks[index]
            first = own_half if half_block == 0 else 1 - own_half
            rows_of = pl.ds(pl.multiple_of(first * half, half), half)
            return ref.at[rows_of, pl.ds(column, width)]

        moves = []

        def move(source, target):
            moves.append(pltpu.make_async_copy(source, target, sems.at[len(moves)]))
            moves[-1].start()

        for index in entering:
            at, slot = slots[index]
            move(region(whole_refs["weight"], index), sends[at].at[slot])
        for (_, source, first, last), target in zip(handing, handed):
            ref = whole_refs["blocks"] if source is None else ins[source]
            move(ref.at[pl.ds(first, last - first)], target)
        for key, mine, other in making:
            one, two = [ins[at][row] for at, row in (mine, other)]
            depth = one.shape[0]
            for side in range(2):
                low, high = (one, two) if side == 0 else (two, one)
                span = pl.ds(side * depth, depth)
                made[key][0, span], made[key][1, span] = two_terms(jnp.where(low_core, low, high))
        for index, stage in tasks:
            if stage > 0:
                mine, theirs = [two_terms(ins[at][slot]) for at, slot in held[index]]
                if stage == stages:
                    target = result_of[index]
                else:
                    at, slot = slots[index]
                    target = sends[at].at[slot]
                key = (chunks[index][0], stage - 1)
                target[...] = product(ins[taken[key]] if key in taken else made[key], mine, theirs)
                if stage == stages:
                    move(target, region(merged_ref, index))
        for each in moves:
            each.wait()

    shape = lambda *dims: jax.ShapeDtypeStruct(dims, jnp.float32)
    outs = [shape(units, half, width) for width, _, units in arrays]
    outs += [shape(last - first, *blocks.shape[1:]) for _, _, first, last in handing]
    outs += [jax.ShapeDtypeStruct((2, half, 2 * half), jnp.bfloat16)] * len(making)
    hbm = pl.BlockSpec(memory_space=pltpu.HBM)
    vmem = pl.BlockSpec(memory_space=pltpu.VMEM)
    room = 62 if merged is None else 40
    merged, *new = pl.pallas_call(
        kernel,
        out_shape=[shape(*weight.shape)] + outs,
        in_specs=[hbm] * len(whole) + [vmem] * len(operands.arrays),
        out_specs=[hbm] + [vmem] * len(outs),
        scratch_shapes=[pltpu.VMEM((half, chunks[index][2]), jnp.float32) for index in leaving]
        + [pltpu.SemaphoreType.DMA((len(entering) + len(handing) + len(leaving) + 1,))],
        input_output_aliases={len(whole) - 1: 0} if merged is not None else {},
        compiler_params=pltpu.CompilerParams(vmem_limit_bytes=room * 2**20),
        cost_estimate=pl.CostEstimate(flops=1, bytes_accessed=1, transcendentals=0),
    )(*whole.values(), *operands.arrays)
    sent, new = new[: len(arrays)], new[len(arrays) :]
    handed, new = dict(zip([hand[0] for hand in handing], new)), new[len(handing) :]
    made = dict(zip([key for key, _, _ in making], new))
    ways = [way for _, way, _ in arrays]
    return merged, sent, ways, slots, handed, made


def pipelined(weight, blocks):
    count, columns = lax.axis_size("row"), lax.axis_size("col")
    bit_count = count.bit_length() - 1
    from_core = lambda array: lax.ppermute(array, "col", partner_route(columns, 1))
    from_across = lambda array: lax.ppermute(array, "col", partner_route(columns, 2))
    chunks, column = [], [0, 0]
    for half_block, eighths in CHUNKS:
        width = weight.shape[1] * eighths // EIGHTHS
        chunks.append((half_block, column[half_block], width))
        column[half_block] += width
    rows = {"blocks": blocks, "cores": from_core(blocks)}
    merged, state, tables = None, {}, {}
    for tasks, work in STEPS:
        merged, sent, ways, slots, handed, made = step(
            weight, blocks, merged, state, tables, rows, tasks, work, chunks, bit_count
        )
        tables.update(made)
        came = [
            lax.ppermute(array, "row", partner_route(count, 1 << way))
            for array, way in zip(sent, ways)
        ]
        for index, (at, slot) in slots.items():
            state[index] = ((sent[at], slot), (came[at], slot))
        for name, array in handed.items():
            rows[name] = from_across(array) if name == ACROSS else from_core(array)
    return merged


def plain(weight, blocks):
    count = lax.axis_size("row")
    bit_count = count.bit_length() - 1
    factors = blocks.shape[0]
    half = blocks.shape[2] // 2
    halves = weight.shape[0] // half
    tables = [lax.all_gather(blocks[k], "col", axis=0, tiled=True) for k in range(factors)]
    bands = []
    for t in range(halves):
        rows = slice(t * half, (t + 1) * half)
        held = weight[rows]
        for factor in range(factors):
            table = tables[factor][rows]
            partner = lax.ppermute(held, "row", partner_route(count, 1 << factor % bit_count))
            dot = functools.partial(jnp.dot, precision=lax.Precision.HIGHEST)
            held = dot(table[:, :half], held) + dot(table[:, half:], partner)
        bands.append(held)
    return jnp.concatenate(bands, axis=0)


def body(weight, blocks):
    fits = lax.axis_size("row") == 8 and lax.axis_size("col") == 4 and blocks.shape[0] == 5
    fits = fits and weight.shape[0] == blocks.shape[2] == 4 * blocks.shape[1]
    fits = fits and weight.shape[1] % (128 * EIGHTHS) == 0
    return (pipelined if fits else plain)(weight, blocks)


def solution(mesh):
    return jax.shard_map(
        body,
        mesh=mesh,
        in_specs=(P("row", "col"), P(None, ("row", "col"), None)),
        out_specs=P("row", "col"),
        check_vma=False,
    )
```

```python
import functools

import jax
import jax.numpy as jnp
from jax import lax
from jax.experimental import pallas as pl
from jax.experimental.pallas import tpu as pltpu
from jax.sharding import PartitionSpec as P

CHUNKS = ((0, 2), (0, 2), (0, 2), (0, 2), (1, 2), (1, 2), (1, 2), (1, 2))
EIGHTHS = 8
STEPS = (
    (((0, 0),), ("across",)),
    (((2, 0),), ()),
    (((1, 0),), ("near01", "near24")),
    (((0, 1),), ()),
    (((5, 0), (1, 1)), ()),
    (((0, 2), (4, 0), (3, 0)), ()),
    (((1, 2), (2, 1)), ()),
    (((0, 3), (3, 1), (2, 2)), ()),
    (((1, 3), (0, 4)), ("cs0",)),
    (((3, 2),), ()),
    (((2, 3), (6, 0), (1, 4), (5, 1)), ("mk0", "cs2")),
    (((3, 3), (0, 5), (4, 1)), ("cs1", "cs3", "cs4")),
    (((2, 4), (6, 1)), ()),
    (((5, 2),), ("mk1", "mk3")),
    (((7, 0), (4, 2)), ()),
    (((5, 3), (1, 5)), ("mk2",)),
    (((7, 1),), ()),
    (((3, 4), (6, 2), (4, 3), (5, 4)), ()),
    (((7, 2),), ("mk4",)),
    (((6, 3),), ()),
    (((4, 4),), ()),
    (((7, 3),), ()),
    (((6, 4), (3, 5)), ()),
    (((2, 5), (4, 5)), ()),
    (((7, 4),), ()),
    (((5, 5), (6, 5)), ()),
    (((7, 5),), ()),
)
NEAR = {"near01": (0, 2), "near24": (2, 5)}
ACROSS = "across"
SHARE = {"cs0": 0, "cs1": 1, "cs2": 2, "cs3": 3, "cs4": 4}
FAR = {"mk0": "cs0", "mk1": "cs1", "mk2": "cs2", "mk3": "cs3", "mk4": "cs4"}


def partner_route(count, mask):
    return [(low, low ^ mask) for low in range(count) if low ^ mask < count]


def two_terms(values):
    high = values.astype(jnp.bfloat16)
    return high, (values - high.astype(jnp.float32)).astype(jnp.bfloat16)


def product(table, first, second):
    high = jnp.concatenate([first[0], second[0]], axis=0)
    low = jnp.concatenate([first[1], second[1]], axis=0)
    dot = functools.partial(jnp.dot, preferred_element_type=jnp.float32)
    return dot(table[0], high) + (dot(table[0], low) + dot(table[1], high))


class Operands:
    def __init__(self):
        self.arrays, self.places = [], {}

    def add(self, array):
        if id(array) not in self.places:
            self.places[id(array)] = len(self.arrays)
            self.arrays.append(array)
        return self.places[id(array)]


def step(weight, blocks, merged, state, tables, rows, tasks, work, chunks, bit_count):
    half = blocks.shape[2] // 2
    stages = blocks.shape[0]
    operands, held, taken = Operands(), {}, {}
    for index, stage in tasks:
        if stage > 0:
            sent, came = state[index]
            held[index] = [(operands.add(sent[0]), sent[1]), (operands.add(came[0]), came[1])]
            key = (chunks[index][0], stage - 1)
            if key in tables:
                taken[key] = operands.add(tables[key])

    making, handing = [], []
    for name in work:
        if name in NEAR:
            mine, other = [operands.add(rows[n]) for n in ("blocks", "cores")]
            making += [((0, k), (mine, k), (other, k)) for k in range(*NEAR[name])]
        elif name in FAR:
            k = SHARE[FAR[name]]
            mine, other = operands.add(rows[ACROSS]), operands.add(rows[FAR[name]])
            making.append(((1, k), (mine, k), (other, 0)))
        elif name == ACROSS:
            handing.append((name, None, 0, stages))
        else:
            handing.append((name, operands.add(rows[ACROSS]), SHARE[name], SHARE[name] + 1))

    arrays, slots = [], {}
    for index, stage in tasks:
        if stage < stages:
            way = stage % bit_count
            for at, (width, other, total) in enumerate(arrays):
                if (width, other) == (chunks[index][2], way):
                    break
            else:
                at, total = len(arrays), 0
                arrays.append(None)
            arrays[at] = (chunks[index][2], way, total + 1)
            slots[index] = (at, total)
    entering = [index for index, stage in tasks if stage == 0]
    leaving = [index for index, stage in tasks if stage == stages]
    whole = {}
    if entering:
        whole["weight"] = weight
    if any(source is None for _, source, _, _ in handing):
        whole["blocks"] = blocks
    if merged is not None:
        whole["merged"] = merged

    def kernel(*refs):
        whole_refs, refs = dict(zip(whole, refs)), refs[len(whole) :]
        ins, refs = refs[: len(operands.arrays)], refs[len(operands.arrays) :]
        merged_ref, refs = refs[0], refs[1:]
        sends, refs = refs[: len(arrays)], refs[len(arrays) :]
        handed, refs = refs[: len(handing)], refs[len(handing) :]
        made, refs = dict(zip([key for key, _, _ in making], refs)), refs[len(making) :]
        result_of, sems = dict(zip(leaving, refs)), refs[len(leaving)]
        col = lax.axis_index("col")
        own_half, low_core = col // 2, col % 2 == 0

        def region(ref, index):
            half_block, column, width = chunks[index]
            first = own_half if half_block == 0 else 1 - own_half
            rows_of = pl.ds(pl.multiple_of(first * half, half), half)
            return ref.at[rows_of, pl.ds(column, width)]

        moves = []

        def move(source, target):
            moves.append(pltpu.make_async_copy(source, target, sems.at[len(moves)]))
            moves[-1].start()

        for index in entering:
            at, slot = slots[index]
            move(region(whole_refs["weight"], index), sends[at].at[slot])
        for (_, source, first, last), target in zip(handing, handed):
            ref = whole_refs["blocks"] if source is None else ins[source]
            move(ref.at[pl.ds(first, last - first)], target)
        for key, mine, other in making:
            one, two = [ins[at][row] for at, row in (mine, other)]
            depth = one.shape[0]
            for side in range(2):
                low, high = (one, two) if side == 0 else (two, one)
                span = pl.ds(side * depth, depth)
                made[key][0, span], made[key][1, span] = two_terms(jnp.where(low_core, low, high))
        for index, stage in tasks:
            if stage > 0:
                mine, theirs = [two_terms(ins[at][slot]) for at, slot in held[index]]
                if stage == stages:
                    target = result_of[index]
                else:
                    at, slot = slots[index]
                    target = sends[at].at[slot]
                key = (chunks[index][0], stage - 1)
                target[...] = product(ins[taken[key]] if key in taken else made[key], mine, theirs)
                if stage == stages:
                    move(target, region(merged_ref, index))
        for each in moves:
            each.wait()

    shape = lambda *dims: jax.ShapeDtypeStruct(dims, jnp.float32)
    outs = [shape(units, half, width) for width, _, units in arrays]
    outs += [shape(last - first, *blocks.shape[1:]) for _, _, first, last in handing]
    outs += [jax.ShapeDtypeStruct((2, half, 2 * half), jnp.bfloat16)] * len(making)
    hbm = pl.BlockSpec(memory_space=pltpu.HBM)
    vmem = pl.BlockSpec(memory_space=pltpu.VMEM)
    room = 60 if merged is None else 40
    merged, *new = pl.pallas_call(
        kernel,
        out_shape=[shape(*weight.shape)] + outs,
        in_specs=[hbm] * len(whole) + [vmem] * len(operands.arrays),
        out_specs=[hbm] + [vmem] * len(outs),
        scratch_shapes=[pltpu.VMEM((half, chunks[index][2]), jnp.float32) for index in leaving]
        + [pltpu.SemaphoreType.DMA((len(entering) + len(handing) + len(leaving) + 1,))],
        input_output_aliases={len(whole) - 1: 0} if merged is not None else {},
        compiler_params=pltpu.CompilerParams(vmem_limit_bytes=room * 2**20),
        cost_estimate=pl.CostEstimate(flops=1, bytes_accessed=1, transcendentals=0),
    )(*whole.values(), *operands.arrays)
    sent, new = new[: len(arrays)], new[len(arrays) :]
    handed, new = dict(zip([hand[0] for hand in handing], new)), new[len(handing) :]
    made = dict(zip([key for key, _, _ in making], new))
    ways = [way for _, way, _ in arrays]
    return merged, sent, ways, slots, handed, made


def pipelined(weight, blocks):
    count, columns = lax.axis_size("row"), lax.axis_size("col")
    bit_count = count.bit_length() - 1
    from_core = lambda array: lax.ppermute(array, "col", partner_route(columns, 1))
    from_across = lambda array: lax.ppermute(array, "col", partner_route(columns, 2))
    chunks, column = [], [0, 0]
    for half_block, eighths in CHUNKS:
        width = weight.shape[1] * eighths // EIGHTHS
        chunks.append((half_block, column[half_block], width))
        column[half_block] += width
    rows = {"blocks": blocks, "cores": from_core(blocks)}
    merged, state, tables = None, {}, {}
    for tasks, work in STEPS:
        merged, sent, ways, slots, handed, made = step(
            weight, blocks, merged, state, tables, rows, tasks, work, chunks, bit_count
        )
        tables.update(made)
        came = [
            lax.ppermute(array, "row", partner_route(count, 1 << way))
            for array, way in zip(sent, ways)
        ]
        for index, (at, slot) in slots.items():
            state[index] = ((sent[at], slot), (came[at], slot))
        for name, array in handed.items():
            rows[name] = from_across(array) if name == ACROSS else from_core(array)
    return merged


def plain(weight, blocks):
    count = lax.axis_size("row")
    bit_count = count.bit_length() - 1
    factors = blocks.shape[0]
    half = blocks.shape[2] // 2
    halves = weight.shape[0] // half
    tables = [lax.all_gather(blocks[k], "col", axis=0, tiled=True) for k in range(factors)]
    bands = []
    for t in range(halves):
        rows = slice(t * half, (t + 1) * half)
        held = weight[rows]
        for factor in range(factors):
            table = tables[factor][rows]
            partner = lax.ppermute(held, "row", partner_route(count, 1 << factor % bit_count))
            dot = functools.partial(jnp.dot, precision=lax.Precision.HIGHEST)
            held = dot(table[:, :half], held) + dot(table[:, half:], partner)
        bands.append(held)
    return jnp.concatenate(bands, axis=0)


def body(weight, blocks):
    fits = lax.axis_size("row") == 8 and lax.axis_size("col") == 4 and blocks.shape[0] == 5
    fits = fits and weight.shape[0] == blocks.shape[2] == 4 * blocks.shape[1]
    fits = fits and weight.shape[1] % (128 * EIGHTHS) == 0
    return (pipelined if fits else plain)(weight, blocks)


def solution(mesh):
    return jax.shard_map(
        body,
        mesh=mesh,
        in_specs=(P("row", "col"), P(None, ("row", "col"), None)),
        out_specs=P("row", "col"),
        check_vma=False,
    )
```

```python
import functools

import jax
import jax.numpy as jnp
from jax import lax
from jax.experimental import pallas as pl
from jax.experimental.pallas import tpu as pltpu
from jax.sharding import PartitionSpec as P

CHUNKS = ((0, 2), (0, 2), (0, 2), (0, 2), (1, 2), (1, 2), (1, 2), (1, 2))
EIGHTHS = 8
STEPS = (
    (((0, 0),), ()),
    (((2, 0),), ("across",)),
    (((1, 0),), ("near01", "near24")),
    (((0, 1),), ()),
    (((5, 0), (1, 1)), ()),
    (((0, 2), (4, 0), (3, 0)), ()),
    (((1, 2), (2, 1)), ()),
    (((0, 3), (3, 1), (2, 2)), ()),
    (((1, 3), (0, 4)), ("cs0",)),
    (((3, 2),), ()),
    (((2, 3), (6, 0), (1, 4), (5, 1)), ("mk0", "cs2")),
    (((3, 3), (0, 5), (4, 1)), ("cs1", "cs3", "cs4")),
    (((2, 4), (6, 1)), ()),
    (((5, 2),), ("mk1", "mk3")),
    (((7, 0), (4, 2)), ()),
    (((5, 3), (1, 5)), ("mk2",)),
    (((7, 1),), ()),
    (((3, 4), (6, 2), (4, 3), (5, 4)), ()),
    (((7, 2),), ("mk4",)),
    (((6, 3),), ()),
    (((4, 4),), ()),
    (((7, 3),), ()),
    (((6, 4), (3, 5)), ()),
    (((2, 5), (4, 5)), ()),
    (((7, 4),), ()),
    (((5, 5), (6, 5)), ()),
    (((7, 5),), ()),
)
NEAR = {"near01": (0, 2), "near24": (2, 5)}
ACROSS = "across"
SHARE = {"cs0": 0, "cs1": 1, "cs2": 2, "cs3": 3, "cs4": 4}
FAR = {"mk0": "cs0", "mk1": "cs1", "mk2": "cs2", "mk3": "cs3", "mk4": "cs4"}


def partner_route(count, mask):
    return [(low, low ^ mask) for low in range(count) if low ^ mask < count]


def two_terms(values):
    high = values.astype(jnp.bfloat16)
    return high, (values - high.astype(jnp.float32)).astype(jnp.bfloat16)


def product(table, first, second):
    high = jnp.concatenate([first[0], second[0]], axis=0)
    low = jnp.concatenate([first[1], second[1]], axis=0)
    dot = functools.partial(jnp.dot, preferred_element_type=jnp.float32)
    return dot(table[0], high) + (dot(table[0], low) + dot(table[1], high))


class Operands:
    def __init__(self):
        self.arrays, self.places = [], {}

    def add(self, array):
        if id(array) not in self.places:
            self.places[id(array)] = len(self.arrays)
            self.arrays.append(array)
        return self.places[id(array)]


def step(weight, blocks, merged, state, tables, rows, tasks, work, chunks, bit_count):
    half = blocks.shape[2] // 2
    stages = blocks.shape[0]
    operands, held, taken = Operands(), {}, {}
    for index, stage in tasks:
        if stage > 0:
            sent, came = state[index]
            held[index] = [(operands.add(sent[0]), sent[1]), (operands.add(came[0]), came[1])]
            key = (chunks[index][0], stage - 1)
            if key in tables:
                taken[key] = operands.add(tables[key])

    making, handing = [], []
    for name in work:
        if name in NEAR:
            mine, other = [operands.add(rows[n]) for n in ("blocks", "cores")]
            making += [((0, k), (mine, k), (other, k)) for k in range(*NEAR[name])]
        elif name in FAR:
            k = SHARE[FAR[name]]
            mine, other = operands.add(rows[ACROSS]), operands.add(rows[FAR[name]])
            making.append(((1, k), (mine, k), (other, 0)))
        elif name == ACROSS:
            handing.append((name, None, 0, stages))
        else:
            handing.append((name, operands.add(rows[ACROSS]), SHARE[name], SHARE[name] + 1))

    arrays, slots = [], {}
    for index, stage in tasks:
        if stage < stages:
            way = stage % bit_count
            for at, (width, other, total) in enumerate(arrays):
                if (width, other) == (chunks[index][2], way):
                    break
            else:
                at, total = len(arrays), 0
                arrays.append(None)
            arrays[at] = (chunks[index][2], way, total + 1)
            slots[index] = (at, total)
    entering = [index for index, stage in tasks if stage == 0]
    leaving = [index for index, stage in tasks if stage == stages]
    whole = {}
    if entering:
        whole["weight"] = weight
    if any(source is None for _, source, _, _ in handing):
        whole["blocks"] = blocks
    if merged is not None:
        whole["merged"] = merged

    def kernel(*refs):
        whole_refs, refs = dict(zip(whole, refs)), refs[len(whole) :]
        ins, refs = refs[: len(operands.arrays)], refs[len(operands.arrays) :]
        merged_ref, refs = refs[0], refs[1:]
        sends, refs = refs[: len(arrays)], refs[len(arrays) :]
        handed, refs = refs[: len(handing)], refs[len(handing) :]
        made, refs = dict(zip([key for key, _, _ in making], refs)), refs[len(making) :]
        result_of, sems = dict(zip(leaving, refs)), refs[len(leaving)]
        col = lax.axis_index("col")
        own_half, low_core = col // 2, col % 2 == 0

        def region(ref, index):
            half_block, column, width = chunks[index]
            first = own_half if half_block == 0 else 1 - own_half
            rows_of = pl.ds(pl.multiple_of(first * half, half), half)
            return ref.at[rows_of, pl.ds(column, width)]

        moves = []

        def move(source, target):
            moves.append(pltpu.make_async_copy(source, target, sems.at[len(moves)]))
            moves[-1].start()

        for index in entering:
            at, slot = slots[index]
            move(region(whole_refs["weight"], index), sends[at].at[slot])
        for (_, source, first, last), target in zip(handing, handed):
            ref = whole_refs["blocks"] if source is None else ins[source]
            move(ref.at[pl.ds(first, last - first)], target)
        for key, mine, other in making:
            one, two = [ins[at][row] for at, row in (mine, other)]
            depth = one.shape[0]
            for side in range(2):
                low, high = (one, two) if side == 0 else (two, one)
                span = pl.ds(side * depth, depth)
                made[key][0, span], made[key][1, span] = two_terms(jnp.where(low_core, low, high))
        for index, stage in tasks:
            if stage > 0:
                mine, theirs = [two_terms(ins[at][slot]) for at, slot in held[index]]
                if stage == stages:
                    target = result_of[index]
                else:
                    at, slot = slots[index]
                    target = sends[at].at[slot]
                key = (chunks[index][0], stage - 1)
                target[...] = product(ins[taken[key]] if key in taken else made[key], mine, theirs)
                if stage == stages:
                    move(target, region(merged_ref, index))
        for each in moves:
            each.wait()

    shape = lambda *dims: jax.ShapeDtypeStruct(dims, jnp.float32)
    outs = [shape(units, half, width) for width, _, units in arrays]
    outs += [shape(last - first, *blocks.shape[1:]) for _, _, first, last in handing]
    outs += [jax.ShapeDtypeStruct((2, half, 2 * half), jnp.bfloat16)] * len(making)
    hbm = pl.BlockSpec(memory_space=pltpu.HBM)
    vmem = pl.BlockSpec(memory_space=pltpu.VMEM)
    room = 52 if merged is None else 40
    merged, *new = pl.pallas_call(
        kernel,
        out_shape=[shape(*weight.shape)] + outs,
        in_specs=[hbm] * len(whole) + [vmem] * len(operands.arrays),
        out_specs=[hbm] + [vmem] * len(outs),
        scratch_shapes=[pltpu.VMEM((half, chunks[index][2]), jnp.float32) for index in leaving]
        + [pltpu.SemaphoreType.DMA((len(entering) + len(handing) + len(leaving) + 1,))],
        input_output_aliases={len(whole) - 1: 0} if merged is not None else {},
        compiler_params=pltpu.CompilerParams(vmem_limit_bytes=room * 2**20),
        cost_estimate=pl.CostEstimate(flops=1, bytes_accessed=1, transcendentals=0),
    )(*whole.values(), *operands.arrays)
    sent, new = new[: len(arrays)], new[len(arrays) :]
    handed, new = dict(zip([hand[0] for hand in handing], new)), new[len(handing) :]
    made = dict(zip([key for key, _, _ in making], new))
    ways = [way for _, way, _ in arrays]
    return merged, sent, ways, slots, handed, made


def pipelined(weight, blocks):
    count, columns = lax.axis_size("row"), lax.axis_size("col")
    bit_count = count.bit_length() - 1
    from_core = lambda array: lax.ppermute(array, "col", partner_route(columns, 1))
    from_across = lambda array: lax.ppermute(array, "col", partner_route(columns, 2))
    chunks, column = [], [0, 0]
    for half_block, eighths in CHUNKS:
        width = weight.shape[1] * eighths // EIGHTHS
        chunks.append((half_block, column[half_block], width))
        column[half_block] += width
    rows = {"blocks": blocks, "cores": from_core(blocks)}
    merged, state, tables = None, {}, {}
    for tasks, work in STEPS:
        merged, sent, ways, slots, handed, made = step(
            weight, blocks, merged, state, tables, rows, tasks, work, chunks, bit_count
        )
        tables.update(made)
        came = [
            lax.ppermute(array, "row", partner_route(count, 1 << way))
            for array, way in zip(sent, ways)
        ]
        for index, (at, slot) in slots.items():
            state[index] = ((sent[at], slot), (came[at], slot))
        for name, array in handed.items():
            rows[name] = from_across(array) if name == ACROSS else from_core(array)
    return merged


def plain(weight, blocks):
    count = lax.axis_size("row")
    bit_count = count.bit_length() - 1
    factors = blocks.shape[0]
    half = blocks.shape[2] // 2
    halves = weight.shape[0] // half
    tables = [lax.all_gather(blocks[k], "col", axis=0, tiled=True) for k in range(factors)]
    bands = []
    for t in range(halves):
        rows = slice(t * half, (t + 1) * half)
        held = weight[rows]
        for factor in range(factors):
            table = tables[factor][rows]
            partner = lax.ppermute(held, "row", partner_route(count, 1 << factor % bit_count))
            dot = functools.partial(jnp.dot, precision=lax.Precision.HIGHEST)
            held = dot(table[:, :half], held) + dot(table[:, half:], partner)
        bands.append(held)
    return jnp.concatenate(bands, axis=0)


def body(weight, blocks):
    fits = lax.axis_size("row") == 8 and lax.axis_size("col") == 4 and blocks.shape[0] == 5
    fits = fits and weight.shape[0] == blocks.shape[2] == 4 * blocks.shape[1]
    fits = fits and weight.shape[1] % (128 * EIGHTHS) == 0
    return (pipelined if fits else plain)(weight, blocks)


def solution(mesh):
    return jax.shard_map(
        body,
        mesh=mesh,
        in_specs=(P("row", "col"), P(None, ("row", "col"), None)),
        out_specs=P("row", "col"),
        check_vma=False,
    )
```

```python
import functools

import jax
import jax.numpy as jnp
from jax import lax
from jax.experimental import pallas as pl
from jax.experimental.pallas import tpu as pltpu
from jax.sharding import PartitionSpec as P

CHUNKS = ((0, 2), (0, 2), (0, 2), (0, 2), (1, 2), (1, 2), (1, 2), (1, 2))
EIGHTHS = 8
STEPS = (
    (((0, 0),), ()),
    (((2, 0),), ("across",)),
    (((1, 0),), ("near01", "near24")),
    (((0, 1),), ()),
    (((5, 0), (1, 1)), ()),
    (((0, 2), (4, 0), (3, 0)), ()),
    (((1, 2), (2, 1)), ()),
    (((0, 3), (3, 1), (2, 2)), ()),
    (((1, 3), (0, 4)), ("cs0",)),
    (((3, 2),), ()),
    (((2, 3), (6, 0), (1, 4), (5, 1)), ("mk0", "cs2")),
    (((3, 3), (0, 5), (4, 1)), ("cs1", "cs3", "cs4")),
    (((2, 4), (6, 1)), ()),
    (((5, 2),), ("mk1", "mk3")),
    (((7, 0), (4, 2)), ()),
    (((5, 3), (1, 5)), ("mk2",)),
    (((7, 1),), ()),
    (((3, 4), (6, 2), (4, 3), (5, 4)), ()),
    (((7, 2),), ("mk4",)),
    (((6, 3),), ()),
    (((4, 4),), ()),
    (((7, 3),), ()),
    (((6, 4), (3, 5)), ()),
    (((2, 5), (4, 5)), ()),
    (((7, 4),), ()),
    (((5, 5), (6, 5)), ()),
    (((7, 5),), ()),
)
NEAR = {"near01": (0, 2), "near24": (2, 5)}
ACROSS = "across"
SHARE = {"cs0": 0, "cs1": 1, "cs2": 2, "cs3": 3, "cs4": 4}
FAR = {"mk0": "cs0", "mk1": "cs1", "mk2": "cs2", "mk3": "cs3", "mk4": "cs4"}


def partner_route(count, mask):
    return [(low, low ^ mask) for low in range(count) if low ^ mask < count]


def two_terms(values):
    high = values.astype(jnp.bfloat16)
    return high, (values - high.astype(jnp.float32)).astype(jnp.bfloat16)


def product(table, first, second):
    high = jnp.concatenate([first[0], second[0]], axis=0)
    low = jnp.concatenate([first[1], second[1]], axis=0)
    dot = functools.partial(jnp.dot, preferred_element_type=jnp.float32)
    return dot(table[0], high) + (dot(table[0], low) + dot(table[1], high))


class Operands:
    def __init__(self):
        self.arrays, self.places = [], {}

    def add(self, array):
        if id(array) not in self.places:
            self.places[id(array)] = len(self.arrays)
            self.arrays.append(array)
        return self.places[id(array)]


def step(weight, blocks, merged, state, tables, rows, tasks, work, chunks, bit_count):
    half = blocks.shape[2] // 2
    stages = blocks.shape[0]
    operands, held, taken = Operands(), {}, {}
    for index, stage in tasks:
        if stage > 0:
            sent, came = state[index]
            held[index] = [(operands.add(sent[0]), sent[1]), (operands.add(came[0]), came[1])]
            key = (chunks[index][0], stage - 1)
            if key in tables:
                taken[key] = operands.add(tables[key])

    making, handing = [], []
    for name in work:
        if name in NEAR:
            mine, other = [operands.add(rows[n]) for n in ("blocks", "cores")]
            making += [((0, k), (mine, k), (other, k)) for k in range(*NEAR[name])]
        elif name in FAR:
            k = SHARE[FAR[name]]
            mine, other = operands.add(rows[ACROSS]), operands.add(rows[FAR[name]])
            making.append(((1, k), (mine, k), (other, 0)))
        elif name == ACROSS:
            handing.append((name, None, 0, stages))
        else:
            handing.append((name, operands.add(rows[ACROSS]), SHARE[name], SHARE[name] + 1))

    arrays, slots = [], {}
    for index, stage in tasks:
        if stage < stages:
            way = stage % bit_count
            for at, (width, other, total) in enumerate(arrays):
                if (width, other) == (chunks[index][2], way):
                    break
            else:
                at, total = len(arrays), 0
                arrays.append(None)
            arrays[at] = (chunks[index][2], way, total + 1)
            slots[index] = (at, total)
    entering = [index for index, stage in tasks if stage == 0]
    leaving = [index for index, stage in tasks if stage == stages]
    whole = {}
    if entering:
        whole["weight"] = weight
    if any(source is None for _, source, _, _ in handing):
        whole["blocks"] = blocks
    if merged is not None:
        whole["merged"] = merged

    def kernel(*refs):
        whole_refs, refs = dict(zip(whole, refs)), refs[len(whole) :]
        ins, refs = refs[: len(operands.arrays)], refs[len(operands.arrays) :]
        merged_ref, refs = refs[0], refs[1:]
        sends, refs = refs[: len(arrays)], refs[len(arrays) :]
        handed, refs = refs[: len(handing)], refs[len(handing) :]
        made, refs = dict(zip([key for key, _, _ in making], refs)), refs[len(making) :]
        result_of, sems = dict(zip(leaving, refs)), refs[len(leaving)]
        col = lax.axis_index("col")
        own_half, low_core = col // 2, col % 2 == 0

        def region(ref, index):
            half_block, column, width = chunks[index]
            first = own_half if half_block == 0 else 1 - own_half
            rows_of = pl.ds(pl.multiple_of(first * half, half), half)
            return ref.at[rows_of, pl.ds(column, width)]

        moves = []

        def move(source, target):
            moves.append(pltpu.make_async_copy(source, target, sems.at[len(moves)]))
            moves[-1].start()

        for index in entering:
            at, slot = slots[index]
            move(region(whole_refs["weight"], index), sends[at].at[slot])
        for (_, source, first, last), target in zip(handing, handed):
            ref = whole_refs["blocks"] if source is None else ins[source]
            move(ref.at[pl.ds(first, last - first)], target)
        for key, mine, other in making:
            one, two = [ins[at][row] for at, row in (mine, other)]
            depth = one.shape[0]
            for side in range(2):
                low, high = (one, two) if side == 0 else (two, one)
                span = pl.ds(side * depth, depth)
                made[key][0, span], made[key][1, span] = two_terms(jnp.where(low_core, low, high))
        for index, stage in tasks:
            if stage > 0:
                mine, theirs = [two_terms(ins[at][slot]) for at, slot in held[index]]
                if stage == stages:
                    target = result_of[index]
                else:
                    at, slot = slots[index]
                    target = sends[at].at[slot]
                key = (chunks[index][0], stage - 1)
                table = ins[taken[key]] if key in taken else made[key]
                if stage < stages:
                    target[...] = product(table, mine, theirs)
                    continue
                place = region(merged_ref, index)
                for first in range(0, half, half // 2):
                    span = pl.ds(first, half // 2)
                    target[span] = product(table.at[:, span], mine, theirs)
                    move(target.at[span], place.at[span])
        for each in moves:
            each.wait()

    shape = lambda *dims: jax.ShapeDtypeStruct(dims, jnp.float32)
    outs = [shape(units, half, width) for width, _, units in arrays]
    outs += [shape(last - first, *blocks.shape[1:]) for _, _, first, last in handing]
    outs += [jax.ShapeDtypeStruct((2, half, 2 * half), jnp.bfloat16)] * len(making)
    hbm = pl.BlockSpec(memory_space=pltpu.HBM)
    vmem = pl.BlockSpec(memory_space=pltpu.VMEM)
    room = 52 if merged is None else 40
    merged, *new = pl.pallas_call(
        kernel,
        out_shape=[shape(*weight.shape)] + outs,
        in_specs=[hbm] * len(whole) + [vmem] * len(operands.arrays),
        out_specs=[hbm] + [vmem] * len(outs),
        scratch_shapes=[pltpu.VMEM((half, chunks[index][2]), jnp.float32) for index in leaving]
        + [pltpu.SemaphoreType.DMA((len(entering) + len(handing) + 2 * len(leaving) + 1,))],
        input_output_aliases={len(whole) - 1: 0} if merged is not None else {},
        compiler_params=pltpu.CompilerParams(vmem_limit_bytes=room * 2**20),
        cost_estimate=pl.CostEstimate(flops=1, bytes_accessed=1, transcendentals=0),
    )(*whole.values(), *operands.arrays)
    sent, new = new[: len(arrays)], new[len(arrays) :]
    handed, new = dict(zip([hand[0] for hand in handing], new)), new[len(handing) :]
    made = dict(zip([key for key, _, _ in making], new))
    ways = [way for _, way, _ in arrays]
    return merged, sent, ways, slots, handed, made


def pipelined(weight, blocks):
    count, columns = lax.axis_size("row"), lax.axis_size("col")
    bit_count = count.bit_length() - 1
    from_core = lambda array: lax.ppermute(array, "col", partner_route(columns, 1))
    from_across = lambda array: lax.ppermute(array, "col", partner_route(columns, 2))
    chunks, column = [], [0, 0]
    for half_block, eighths in CHUNKS:
        width = weight.shape[1] * eighths // EIGHTHS
        chunks.append((half_block, column[half_block], width))
        column[half_block] += width
    rows = {"blocks": blocks, "cores": from_core(blocks)}
    merged, state, tables = None, {}, {}
    for tasks, work in STEPS:
        merged, sent, ways, slots, handed, made = step(
            weight, blocks, merged, state, tables, rows, tasks, work, chunks, bit_count
        )
        tables.update(made)
        came = [
            lax.ppermute(array, "row", partner_route(count, 1 << way))
            for array, way in zip(sent, ways)
        ]
        for index, (at, slot) in slots.items():
            state[index] = ((sent[at], slot), (came[at], slot))
        for name, array in handed.items():
            rows[name] = from_across(array) if name == ACROSS else from_core(array)
    return merged


def plain(weight, blocks):
    count = lax.axis_size("row")
    bit_count = count.bit_length() - 1
    factors = blocks.shape[0]
    half = blocks.shape[2] // 2
    halves = weight.shape[0] // half
    tables = [lax.all_gather(blocks[k], "col", axis=0, tiled=True) for k in range(factors)]
    bands = []
    for t in range(halves):
        rows = slice(t * half, (t + 1) * half)
        held = weight[rows]
        for factor in range(factors):
            table = tables[factor][rows]
            partner = lax.ppermute(held, "row", partner_route(count, 1 << factor % bit_count))
            dot = functools.partial(jnp.dot, precision=lax.Precision.HIGHEST)
            held = dot(table[:, :half], held) + dot(table[:, half:], partner)
        bands.append(held)
    return jnp.concatenate(bands, axis=0)


def body(weight, blocks):
    fits = lax.axis_size("row") == 8 and lax.axis_size("col") == 4 and blocks.shape[0] == 5
    fits = fits and weight.shape[0] == blocks.shape[2] == 4 * blocks.shape[1]
    fits = fits and weight.shape[1] % (128 * EIGHTHS) == 0
    return (pipelined if fits else plain)(weight, blocks)


def solution(mesh):
    return jax.shard_map(
        body,
        mesh=mesh,
        in_specs=(P("row", "col"), P(None, ("row", "col"), None)),
        out_specs=P("row", "col"),
        check_vma=False,
    )
```

```python
import functools

import jax
import jax.numpy as jnp
from jax import lax
from jax.experimental import pallas as pl
from jax.experimental.pallas import tpu as pltpu
from jax.sharding import PartitionSpec as P

CHUNKS = ((0, 2), (0, 2), (0, 2), (0, 2), (1, 2), (1, 2), (1, 2), (1, 2))
EIGHTHS = 8
STEPS = (
    (((0, 0),), ()),
    (((2, 0),), ("across",)),
    (((1, 0),), ("near01",)),
    (((0, 1),), ()),
    (((5, 0), (1, 1)), ("near24",)),
    (((0, 2), (4, 0), (3, 0)), ()),
    (((1, 2), (2, 1)), ()),
    (((0, 3), (3, 1), (2, 2)), ()),
    (((1, 3), (0, 4)), ("cs0",)),
    (((3, 2),), ()),
    (((2, 3), (6, 0), (1, 4), (5, 1)), ("mk0", "cs2")),
    (((3, 3), (0, 5), (4, 1)), ("cs1", "cs3", "cs4")),
    (((2, 4), (6, 1)), ()),
    (((5, 2),), ("mk1", "mk3")),
    (((7, 0), (4, 2)), ()),
    (((5, 3), (1, 5)), ("mk2",)),
    (((7, 1),), ()),
    (((3, 4), (6, 2), (4, 3), (5, 4)), ()),
    (((7, 2),), ("mk4",)),
    (((6, 3),), ()),
    (((4, 4),), ()),
    (((7, 3),), ()),
    (((6, 4), (3, 5)), ()),
    (((2, 5), (4, 5)), ()),
    (((7, 4),), ()),
    (((5, 5), (6, 5)), ()),
    (((7, 5),), ()),
)
NEAR = {"near01": (0, 2), "near24": (2, 5)}
ACROSS = "across"
SHARE = {"cs0": 0, "cs1": 1, "cs2": 2, "cs3": 3, "cs4": 4}
FAR = {"mk0": "cs0", "mk1": "cs1", "mk2": "cs2", "mk3": "cs3", "mk4": "cs4"}


def partner_route(count, mask):
    return [(low, low ^ mask) for low in range(count) if low ^ mask < count]


def two_terms(values):
    high = values.astype(jnp.bfloat16)
    return high, (values - high.astype(jnp.float32)).astype(jnp.bfloat16)


def product(table, first, second):
    high = jnp.concatenate([first[0], second[0]], axis=0)
    low = jnp.concatenate([first[1], second[1]], axis=0)
    dot = functools.partial(jnp.dot, preferred_element_type=jnp.float32)
    return dot(table[0], high) + (dot(table[0], low) + dot(table[1], high))


class Operands:
    def __init__(self):
        self.arrays, self.places = [], {}

    def add(self, array):
        if id(array) not in self.places:
            self.places[id(array)] = len(self.arrays)
            self.arrays.append(array)
        return self.places[id(array)]


def step(weight, blocks, merged, state, tables, rows, tasks, work, chunks, bit_count):
    half = blocks.shape[2] // 2
    stages = blocks.shape[0]
    operands, held, taken = Operands(), {}, {}
    for index, stage in tasks:
        if stage > 0:
            sent, came = state[index]
            held[index] = [(operands.add(sent[0]), sent[1]), (operands.add(came[0]), came[1])]
            key = (chunks[index][0], stage - 1)
            if key in tables:
                taken[key] = operands.add(tables[key])

    making, handing = [], []
    for name in work:
        if name in NEAR:
            mine, other = [operands.add(rows[n]) for n in ("blocks", "cores")]
            making += [((0, k), (mine, k), (other, k)) for k in range(*NEAR[name])]
        elif name in FAR:
            k = SHARE[FAR[name]]
            mine, other = operands.add(rows[ACROSS]), operands.add(rows[FAR[name]])
            making.append(((1, k), (mine, k), (other, 0)))
        elif name == ACROSS:
            handing.append((name, None, 0, stages))
        else:
            handing.append((name, operands.add(rows[ACROSS]), SHARE[name], SHARE[name] + 1))

    arrays, slots = [], {}
    for index, stage in tasks:
        if stage < stages:
            way = stage % bit_count
            for at, (width, other, total) in enumerate(arrays):
                if (width, other) == (chunks[index][2], way):
                    break
            else:
                at, total = len(arrays), 0
                arrays.append(None)
            arrays[at] = (chunks[index][2], way, total + 1)
            slots[index] = (at, total)
    entering = [index for index, stage in tasks if stage == 0]
    leaving = [index for index, stage in tasks if stage == stages]
    whole = {}
    if entering:
        whole["weight"] = weight
    if any(source is None for _, source, _, _ in handing):
        whole["blocks"] = blocks
    if merged is not None:
        whole["merged"] = merged

    def kernel(*refs):
        whole_refs, refs = dict(zip(whole, refs)), refs[len(whole) :]
        ins, refs = refs[: len(operands.arrays)], refs[len(operands.arrays) :]
        merged_ref, refs = refs[0], refs[1:]
        sends, refs = refs[: len(arrays)], refs[len(arrays) :]
        handed, refs = refs[: len(handing)], refs[len(handing) :]
        made, refs = dict(zip([key for key, _, _ in making], refs)), refs[len(making) :]
        result_of, sems = dict(zip(leaving, refs)), refs[len(leaving)]
        col = lax.axis_index("col")
        own_half, low_core = col // 2, col % 2 == 0

        def region(ref, index):
            half_block, column, width = chunks[index]
            first = own_half if half_block == 0 else 1 - own_half
            rows_of = pl.ds(pl.multiple_of(first * half, half), half)
            return ref.at[rows_of, pl.ds(column, width)]

        moves = []

        def move(source, target):
            moves.append(pltpu.make_async_copy(source, target, sems.at[len(moves)]))
            moves[-1].start()

        for index in entering:
            at, slot = slots[index]
            move(region(whole_refs["weight"], index), sends[at].at[slot])
        for (_, source, first, last), target in zip(handing, handed):
            ref = whole_refs["blocks"] if source is None else ins[source]
            move(ref.at[pl.ds(first, last - first)], target)
        for key, mine, other in making:
            one, two = [ins[at][row] for at, row in (mine, other)]
            depth = one.shape[0]
            for side in range(2):
                low, high = (one, two) if side == 0 else (two, one)
                span = pl.ds(side * depth, depth)
                made[key][0, span], made[key][1, span] = two_terms(jnp.where(low_core, low, high))
        for index, stage in tasks:
            if stage > 0:
                mine, theirs = [two_terms(ins[at][slot]) for at, slot in held[index]]
                if stage == stages:
                    target = result_of[index]
                else:
                    at, slot = slots[index]
                    target = sends[at].at[slot]
                key = (chunks[index][0], stage - 1)
                table = ins[taken[key]] if key in taken else made[key]
                if stage < stages:
                    target[...] = product(table, mine, theirs)
                    continue
                place = region(merged_ref, index)
                for first in range(0, half, half // 2):
                    span = pl.ds(first, half // 2)
                    target[span] = product(table.at[:, span], mine, theirs)
                    move(target.at[span], place.at[span])
        for each in moves:
            each.wait()

    shape = lambda *dims: jax.ShapeDtypeStruct(dims, jnp.float32)
    outs = [shape(units, half, width) for width, _, units in arrays]
    outs += [shape(last - first, *blocks.shape[1:]) for _, _, first, last in handing]
    outs += [jax.ShapeDtypeStruct((2, half, 2 * half), jnp.bfloat16)] * len(making)
    hbm = pl.BlockSpec(memory_space=pltpu.HBM)
    vmem = pl.BlockSpec(memory_space=pltpu.VMEM)
    room = 52 if merged is None else 40
    merged, *new = pl.pallas_call(
        kernel,
        out_shape=[shape(*weight.shape)] + outs,
        in_specs=[hbm] * len(whole) + [vmem] * len(operands.arrays),
        out_specs=[hbm] + [vmem] * len(outs),
        scratch_shapes=[pltpu.VMEM((half, chunks[index][2]), jnp.float32) for index in leaving]
        + [pltpu.SemaphoreType.DMA((len(entering) + len(handing) + 2 * len(leaving) + 1,))],
        input_output_aliases={len(whole) - 1: 0} if merged is not None else {},
        compiler_params=pltpu.CompilerParams(vmem_limit_bytes=room * 2**20),
        cost_estimate=pl.CostEstimate(flops=1, bytes_accessed=1, transcendentals=0),
    )(*whole.values(), *operands.arrays)
    sent, new = new[: len(arrays)], new[len(arrays) :]
    handed, new = dict(zip([hand[0] for hand in handing], new)), new[len(handing) :]
    made = dict(zip([key for key, _, _ in making], new))
    ways = [way for _, way, _ in arrays]
    return merged, sent, ways, slots, handed, made


def pipelined(weight, blocks):
    count, columns = lax.axis_size("row"), lax.axis_size("col")
    bit_count = count.bit_length() - 1
    from_core = lambda array: lax.ppermute(array, "col", partner_route(columns, 1))
    from_across = lambda array: lax.ppermute(array, "col", partner_route(columns, 2))
    chunks, column = [], [0, 0]
    for half_block, eighths in CHUNKS:
        width = weight.shape[1] * eighths // EIGHTHS
        chunks.append((half_block, column[half_block], width))
        column[half_block] += width
    rows = {"blocks": blocks, "cores": from_core(blocks)}
    merged, state, tables = None, {}, {}
    for tasks, work in STEPS:
        merged, sent, ways, slots, handed, made = step(
            weight, blocks, merged, state, tables, rows, tasks, work, chunks, bit_count
        )
        tables.update(made)
        came = [
            lax.ppermute(array, "row", partner_route(count, 1 << way))
            for array, way in zip(sent, ways)
        ]
        for index, (at, slot) in slots.items():
            state[index] = ((sent[at], slot), (came[at], slot))
        for name, array in handed.items():
            rows[name] = from_across(array) if name == ACROSS else from_core(array)
    return merged


def plain(weight, blocks):
    count = lax.axis_size("row")
    bit_count = count.bit_length() - 1
    factors = blocks.shape[0]
    half = blocks.shape[2] // 2
    halves = weight.shape[0] // half
    tables = [lax.all_gather(blocks[k], "col", axis=0, tiled=True) for k in range(factors)]
    bands = []
    for t in range(halves):
        rows = slice(t * half, (t + 1) * half)
        held = weight[rows]
        for factor in range(factors):
            table = tables[factor][rows]
            partner = lax.ppermute(held, "row", partner_route(count, 1 << factor % bit_count))
            dot = functools.partial(jnp.dot, precision=lax.Precision.HIGHEST)
            held = dot(table[:, :half], held) + dot(table[:, half:], partner)
        bands.append(held)
    return jnp.concatenate(bands, axis=0)


def body(weight, blocks):
    fits = lax.axis_size("row") == 8 and lax.axis_size("col") == 4 and blocks.shape[0] == 5
    fits = fits and weight.shape[0] == blocks.shape[2] == 4 * blocks.shape[1]
    fits = fits and weight.shape[1] % (128 * EIGHTHS) == 0
    return (pipelined if fits else plain)(weight, blocks)


def solution(mesh):
    return jax.shard_map(
        body,
        mesh=mesh,
        in_specs=(P("row", "col"), P(None, ("row", "col"), None)),
        out_specs=P("row", "col"),
        check_vma=False,
    )
```
